256 devices in a mesh: space: 8 (over y, core), tm: 32 (over x, z).
Axes of the slice: x: 4, y: 4, z: 8, core: 2. Of those that a mesh axis runs over, the one named last changes fastest.
Arguments:
- snapshots: float32 [8192, 61440], P('tm', 'space'), may hold values from -6 to 6
- closing: float32 [128, 61440], P(None, 'space'), may hold values from -6 to 6
- weights: float32 [61440], P('space'), may hold values from 0.25 to 36, as said below
- bin_index: int32 [64], replicated, may hold values from 0 to 128, as said below
Outputs:
- spectra: float32 [64, 2, 64, 64], P('tm', None, 'space')
The draws below stay inside these ranges and needn't reach their ends.
Inputs may be any that keep to these rules, and one draw needn't show every extreme that they name: `bin_index`: distinct bins. Positive weights.
All inputs are finite; a program needn't handle non-finite values.
Results may differ from the reference program's by a relative error of at most 0.0003.
Values sent between devices are 32-bit elements; how exact they have to be, the bound alone decides.
No kernel may reach another device: no remote copies, remote signals or barrier semaphores. Data moves between devices by JAX's collectives and lax.ppermute only.
A program may use at most 128 MiB of HBM per device.

```python
import jax
import jax.numpy as jnp
from jax import lax

NFFT = 256
NBINS = 64
P_DEV = 7680
EXTRA = 128
NBLK = 64
NT = 8192
NPTS = 61440
N_SPACE = 8


def draw_weights(key, part):
    position = jnp.arange(NPTS, dtype=jnp.float32) / (NPTS - 1)
    roughness = jnp.exp(jax.random.uniform(key, (NPTS,), jnp.float32, jnp.log(0.5), jnp.log(2.0)))
    return roughness * jnp.exp(jnp.log(3.0) * position)


def draw_bin_index(key, part):
    shuffled = jax.random.permutation(jax.random.fold_in(key, 11), NFFT // 2 + 1)
    return shuffled[:NBINS].astype(jnp.int32)


def level_of(key, dims, shards, smallest, high):
    factor_of = 1.0
    for dim, blocks in shards:
        heights = jax.random.uniform(jax.random.fold_in(jax.random.fold_in(key, 6), dim), (blocks,), jnp.float32, smallest / len(shards), high / len(shards))
        factor_of = factor_of * jnp.repeat(jnp.exp(heights), dims[dim] // blocks).reshape((-1,) + (1,) * (len(dims) - 1 - dim))
    return factor_of


def bell_draw(own_key, dims, deviation, reach, shards=(), kind=jnp.bfloat16):
    array = jax.random.normal(own_key, dims, jnp.float32) * deviation
    if len(shards) > 0:
        array = level_of(own_key, dims, shards, -0.22, 0.18) * array
    return jnp.clip(array, min=-reach, max=reach).astype(kind)


def setup_inputs(seed: int = 0) -> dict:
    key_list = jax.random.split(jax.random.key(seed), 5)
    snapshots = bell_draw(key_list[0], (NT, NPTS), 1.0, 6.0, ((0, 32), (1, 8)), jnp.float32)
    closing = bell_draw(key_list[1], (EXTRA, NPTS), 1.0, 6.0, ((1, 8),), jnp.float32)
    weights = draw_weights(jax.random.fold_in(key_list[4], 71), 0)
    bin_index = draw_bin_index(jax.random.fold_in(key_list[4], 71), 0)
    return {"snapshots": snapshots, "closing": closing, "weights": weights, "bin_index": bin_index}


def spectral_table(bin_index, length):
    sample = jnp.arange(length, dtype=jnp.int32)
    window = 0.5 - 0.5 * jnp.cos(2.0 * jnp.pi * sample.astype(jnp.float32) / length)
    phase_turns = (sample[:, None] * bin_index[None, :]) % length
    phase_angle = 2.0 * jnp.pi * phase_turns.astype(jnp.float32) / length
    paired = jnp.stack([window[:, None] * jnp.cos(phase_angle), -window[:, None] * jnp.sin(phase_angle)], axis=2)
    return paired.reshape(length, 2 * bin_index.shape[0])


def cross_spectra(first_set, second_set):
    products = jnp.einsum("kaip,kbjp->kabij", first_set, second_set, precision=lax.Precision.HIGHEST)
    real_part = products[:, 0, 0] + products[:, 1, 1]
    imag_part = products[:, 0, 1] - products[:, 1, 0]
    return jnp.stack([real_part, imag_part], axis=1)


def reference(snapshots, closing, weights, bin_index):
    basis_table = spectral_table(bin_index, NFFT)
    starts = jnp.arange(NBLK, dtype=jnp.int32) * (NFFT // 2)

    def group_sum(running, group_index):
        column_start = (group_index * P_DEV).astype(jnp.int32)
        columns = lax.dynamic_slice_in_dim(snapshots, column_start, P_DEV, 1)
        series = jnp.concatenate([columns, lax.dynamic_slice_in_dim(closing, column_start, P_DEV, 1)], axis=0)
        weight = lax.dynamic_slice_in_dim(weights, column_start, P_DEV, 0)

        def transform(begin_row):
            window_rows = lax.dynamic_slice_in_dim(series, begin_row, NFFT, 0)
            return lax.dot_general(basis_table, window_rows, (((0,), (0,)), ((), ())), precision=lax.Precision.HIGHEST)

        spectrum = lax.map(transform, starts)
        spectrum = spectrum.reshape(NBLK, NBINS, 2, P_DEV).transpose(1, 2, 0, 3)
        return running + cross_spectra(spectrum, spectrum * weight), None

    zeros_start = jnp.zeros((NBINS, 2, NBLK, NBLK), jnp.float32)
    cross_sum, unused = lax.scan(group_sum, zeros_start, jnp.arange(N_SPACE, dtype=jnp.int32))
    energy = jnp.trace(cross_sum[:, 0], axis1=1, axis2=2)
    return cross_sum * (NBLK / energy)[:, None, None, None]
```

```python
import jax
import jax.numpy as jnp
from jax import lax
from jax.experimental import pallas as pl
from jax.experimental.pallas import tpu as pltpu
from jax.sharding import PartitionSpec as P

NFFT = 256
NBINS = 64
HOP = NFFT // 2
BLOCKS = 64
LANES = 128
PTS_TM = 192
F32, BF16 = jnp.float32, jnp.bfloat16
VMEM_BYTES = 50 * 2**20


def split(a):
    hi = a.astype(BF16)
    return hi, (a - hi.astype(F32)).astype(BF16)


def dot3(a, b, dims):
    dg = lambda u, v: lax.dot_general(u, v, (dims, ((), ())), preferred_element_type=F32)
    return dg(a[0], b[0]) + dg(a[0], b[1]) + dg(a[1], b[0])


NN, NT = ((1,), (0,)), ((1,), (1,))


def table_rows(bin_index, length):
    sample = jnp.arange(length, dtype=jnp.int32)
    window = 0.5 - 0.5 * jnp.cos(2.0 * jnp.pi * sample.astype(F32) / length)
    turns = sample[None, :] * bin_index[:, None] % length
    angle = 2.0 * jnp.pi * turns.astype(F32) / length
    paired = jnp.stack([window * jnp.cos(angle), -window * jnp.sin(angle)], axis=1)
    return paired.reshape(2 * bin_index.shape[0], length)


def turn_kernel(x_ref, o_ref):
    o_ref[...] = x_ref[...].T


def turned(x, cols):
    rows, step = x.shape[0], 768
    return pl.pallas_call(
        turn_kernel,
        grid=(cols // step,),
        in_specs=[pl.BlockSpec((rows, step), lambda i: (0, i))],
        out_specs=pl.BlockSpec((step, rows), lambda i: (i, 0)),
        out_shape=jax.ShapeDtypeStruct((cols, rows), F32),
        cost_estimate=pl.CostEstimate(flops=0, bytes_accessed=8 * rows * cols, transcendentals=0),
        compiler_params=pltpu.CompilerParams(vmem_limit_bytes=VMEM_BYTES),
        name="turn_samples",
    )(x)


def lane_tile(a, n):
    return a[:, n * LANES : (n + 1) * LANES]


def coef_kernel(t_ref, x_ref, h_ref, o_ref, s_ref):
    table = split(t_ref[...])
    x = x_ref[...]
    tiles = s_ref.shape[0]
    for e, part in enumerate((x, jnp.concatenate([x[HOP:], h_ref[...]], axis=0))):
        got = dot3(table, split(part), NN)
        for n in range(tiles):
            s_ref.at[n][pl.ds(e, 2 * NBINS, stride=2), :] = lane_tile(got, n)
    for n in range(tiles):
        o_ref[:, n] = s_ref[n].reshape(-1, 8, LANES)


def coefs(table, x, halo, first):
    rows, cols = x.shape[0], x.shape[1] - first
    step = 512
    return pl.pallas_call(
        coef_kernel,
        grid=(cols // step,),
        in_specs=[
            pl.BlockSpec((2 * NBINS, rows), lambda i: (0, 0)),
            pl.BlockSpec((rows, step), lambda i: (0, first // step + i)),
            pl.BlockSpec((HOP, step), lambda i: (0, i)),
        ],
        out_specs=pl.BlockSpec((NBINS // 2, step // LANES, 8, LANES), lambda i: (0, i, 0, 0)),
        out_shape=jax.ShapeDtypeStruct((NBINS // 2, cols // LANES, 8, LANES), F32),
        scratch_shapes=[pltpu.VMEM((step // LANES, 4 * NBINS, LANES), F32)],
        cost_estimate=pl.CostEstimate(
            flops=12 * 2 * NBINS * rows * cols, bytes_accessed=10 * rows * cols, transcendentals=0
        ),
        compiler_params=pltpu.CompilerParams(vmem_limit_bytes=VMEM_BYTES),
        name="coefs_by_bin",
    )(table, x, halo)


def re_im(gram):
    half = gram.shape[0] // 2
    other = pltpu.roll(gram[half:], half, 1)
    lane = lax.broadcasted_iota(jnp.int32, other.shape, 1)
    return gram[:half] + jnp.where(lane < half, other, -other)


def points_kernel(where_ref, t_ref, x_ref, c_ref, w_ref, o_ref, s_ref):
    tm_count, pts = x_ref.shape[0], x_ref.shape[1]
    tiles = s_ref.shape[0]
    table = split(t_ref[...])
    blank = jnp.zeros((tiles * LANES - pts, NFFT), F32)

    def transform(j, samples):
        got = dot3(table, split(jnp.concatenate([samples, blank], axis=0)), NT)
        for n in range(tiles):
            s_ref.at[n][pl.ds(j, 2 * NBINS, stride=BLOCKS), :] = lane_tile(got, n)

    def both(t, following):
        x = x_ref[t]
        transform(2 * t, x)
        transform(2 * t + 1, jnp.concatenate([x[:, HOP:], following], axis=1))

    @pl.loop(0, tm_count - 1)
    def _(t):
        both(t, x_ref[t + 1][:, :HOP])

    both(tm_count - 1, c_ref[...])

    y, core, x_at, z_at = (where_ref[n] for n in range(4))
    weights = w_ref[...]

    @pl.loop(0, NBINS)
    def _(k):
        mine = pl.ds(pl.multiple_of(2 * BLOCKS * k, 2 * BLOCKS), 2 * BLOCKS)
        rows = jnp.concatenate([s_ref[n, mine] for n in range(tiles)], axis=1)
        out = re_im(dot3(split(rows), split(rows * weights), NT))
        xr = lax.rem(k // 16 - x_at + 4, 4)
        zr = lax.rem(lax.rem(k // 2, 8) - z_at + 8, 8)
        for s in range(8):
            cr = lax.rem(s % 2 + core, 2)
            yr = lax.rem(s // 2 - y + 4, 4)
            o_ref[cr, yr, xr, zr, lax.rem(k, 2)] = out[8 * s : 8 * s + 8]


def points_gram(where, table, samples, closing, weights):
    wide = -(-samples.shape[1] // NFFT) * NFFT
    vmem = pl.BlockSpec(memory_space=pltpu.VMEM)
    return pl.pallas_call(
        points_kernel,
        in_specs=[pl.BlockSpec(memory_space=pltpu.SMEM), vmem, vmem, vmem, vmem],
        out_specs=vmem,
        out_shape=jax.ShapeDtypeStruct((2, 4, 4, 8, 2, 8, LANES), F32),
        scratch_shapes=[pltpu.VMEM((wide // LANES, 2 * NBINS * BLOCKS, LANES), F32)],
        cost_estimate=pl.CostEstimate(
            flops=6 * 10**9, bytes_accessed=20 * 10**6, transcendentals=0
        ),
        compiler_params=pltpu.CompilerParams(vmem_limit_bytes=VMEM_BYTES),
        name="points_gram",
    )(where, table, samples, closing, weights)


def bins_kernel(where_ref, a_ref, w_ref, b_ref, o_ref, s_ref):
    tiles = s_ref.shape[0]
    tm_count = a_ref.shape[0] // (8 * tiles)
    for n in range(tiles):
        for c in range(4):
            for e in range(2):
                got = a_ref[pl.ds(8 * n + 2 * c + e, tm_count, stride=8 * tiles), :]
                s_ref.at[n][pl.ds(c * BLOCKS + e, tm_count, stride=2), :] = got
    weights = w_ref[...]
    own = 2 * where_ref[0] + where_ref[1]
    row = lax.broadcasted_iota(jnp.int32, (BLOCKS, LANES), 0)
    lane = lax.broadcasted_iota(jnp.int32, (BLOCKS, LANES), 1)
    traces = []
    for b in range(2):
        mine = pl.ds(2 * BLOCKS * b, 2 * BLOCKS)
        rows = jnp.concatenate([s_ref[n, mine] for n in range(tiles)], axis=1)
        out = re_im(dot3(split(rows), split(rows * weights), NT))
        for s in range(8):
            o_ref[s, b] = out[8 * s : 8 * s + 8]
        others = jnp.where(lane[:8] == row[:8] + 8 * own, b_ref[b], 0.0)
        trace = jnp.sum(jnp.where(lane == row, out, 0.0)) + jnp.sum(others)
        traces.append(trace)
    tile = jnp.where(row[:8] == 0, traces[0], traces[1])
    for s in range(8):
        o_ref[s, 2] = tile


def bins_gram(where, coef, weights, others):
    vmem = pl.BlockSpec(memory_space=pltpu.VMEM)
    return pl.pallas_call(
        bins_kernel,
        in_specs=[pl.BlockSpec(memory_space=pltpu.SMEM), vmem, vmem, vmem],
        out_specs=vmem,
        out_shape=jax.ShapeDtypeStruct((8, 3, 8, LANES), F32),
        scratch_shapes=[pltpu.VMEM((weights.shape[1] // LANES, 4 * BLOCKS, LANES), F32)],
        cost_estimate=pl.CostEstimate(
            flops=5 * 10**8, bytes_accessed=2 * 10**6, transcendentals=0
        ),
        compiler_params=pltpu.CompilerParams(vmem_limit_bytes=VMEM_BYTES),
        name="bins_gram",
    )(where, coef, weights, others)


def norm_kernel(r_ref, b_ref, o_ref):
    total = r_ref[0]
    for s in range(1, 8):
        total = total + r_ref[s]
    for b in range(2):
        out = (total[b] + b_ref[b]) * (BLOCKS / total[2, b : b + 1, :])
        o_ref[b, 0] = out[:, :BLOCKS]
        o_ref[b, 1] = out[:, BLOCKS:]


def normalized(parts, others):
    vmem = pl.BlockSpec(memory_space=pltpu.VMEM)
    return pl.pallas_call(
        norm_kernel,
        in_specs=[vmem, vmem],
        out_specs=vmem,
        out_shape=jax.ShapeDtypeStruct((2, 2, 8, BLOCKS), F32),
        name="normalize",
    )(parts, others)


def by_y(d):
    return [(2 * y + c, 2 * ((y + d) % 4) + c) for y in range(4) for c in range(2)]


def by_x(d):
    return [(8 * x + z, 8 * ((x + d) % 4) + z) for x in range(4) for z in range(8)]


def by_z(d):
    return [(8 * x + z, 8 * x + (z + d) % 8) for x in range(4) for z in range(8)]


def reduced(parts):
    held = parts[0] + lax.ppermute(parts[1], "space", [(s, s ^ 1) for s in range(8)])
    for axis, steps, pairs in (("space", 4, by_y), ("tm", 4, by_x), ("tm", 8, by_z)):
        held = sum([lax.ppermute(held[d], axis, pairs(d)) for d in range(1, steps)], held[0])
    return held


def body(snapshots, closing, weights, bin_index):
    tm_count = lax.axis_size("tm")
    tm, space = lax.axis_index("tm"), lax.axis_index("space")
    where = jnp.stack([space // 2, space % 2, tm // 8, tm % 8]).astype(jnp.int32)
    first = tm_count * PTS_TM
    incoming = lax.ppermute(
        snapshots[:HOP, first:], "tm", [(t, t - 1) for t in range(1, tm_count)]
    )
    sent = turned(snapshots, first).reshape(tm_count, PTS_TM, NFFT)
    samples = lax.all_to_all(sent, "tm", 0, 0, tiled=True)
    table = table_rows(bin_index, NFFT)
    halo = jnp.where(tm == tm_count - 1, closing[:, first:], incoming)
    coef = coefs(table, snapshots, halo, first)
    own_closing = lax.dynamic_slice(closing, (0, tm * PTS_TM), (HOP, PTS_TM)).T
    wide = -(-PTS_TM // NFFT) * NFFT
    own_weights = lax.dynamic_slice(weights, (tm * PTS_TM,), (PTS_TM,))
    own_weights = jnp.pad(own_weights, (0, wide - PTS_TM))[None, :]
    samples, coef, own_closing, own_weights, table = lax.optimization_barrier(
        (samples, coef, own_closing, own_weights, table)
    )
    by_bin = lax.all_to_all(coef, "tm", 0, 0, tiled=True)
    others = reduced(points_gram(where, table, samples, own_closing, own_weights))
    parts = bins_gram(where, by_bin.reshape(-1, LANES), weights[None, first:], others)
    return normalized(lax.all_to_all(parts, "space", 0, 0, tiled=True), others)


def solution(mesh):
    return jax.shard_map(
        body,
        mesh=mesh,
        in_specs=(P("tm", "space"), P(None, "space"), P("space"), P()),
        out_specs=P("tm", None, "space", None),
        check_vma=False,
    )
```

```python
import jax
import jax.numpy as jnp
from jax import lax
from jax.experimental import pallas as pl
from jax.experimental.pallas import tpu as pltpu
from jax.sharding import PartitionSpec as P

NFFT = 256
NBINS = 64
HOP = NFFT // 2
BLOCKS = 64
LANES = 128
PTS_TM = 176
F32, BF16 = jnp.float32, jnp.bfloat16
VMEM_BYTES = 50 * 2**20


def split(a):
    hi = a.astype(BF16)
    return hi, (a - hi.astype(F32)).astype(BF16)


def dot3(a, b, dims):
    dg = lambda u, v: lax.dot_general(u, v, (dims, ((), ())), preferred_element_type=F32)
    return dg(a[0], b[0]) + dg(a[0], b[1]) + dg(a[1], b[0])


NN, NT = ((1,), (0,)), ((1,), (1,))


def table_rows(bin_index, length):
    sample = jnp.arange(length, dtype=jnp.int32)
    window = 0.5 - 0.5 * jnp.cos(2.0 * jnp.pi * sample.astype(F32) / length)
    turns = sample[None, :] * bin_index[:, None] % length
    angle = 2.0 * jnp.pi * turns.astype(F32) / length
    paired = jnp.stack([window * jnp.cos(angle), -window * jnp.sin(angle)], axis=1)
    return paired.reshape(2 * bin_index.shape[0], length)


def turn_kernel(x_ref, w_ref, o_ref):
    o_ref[...] = (x_ref[...] * w_ref[...]).T


def turned(x, roots, cols):
    rows, step = x.shape[0], 512
    return pl.pallas_call(
        turn_kernel,
        grid=(cols // step,),
        in_specs=[
            pl.BlockSpec((rows, step), lambda i: (0, i)),
            pl.BlockSpec((1, step), lambda i: (0, i)),
        ],
        out_specs=pl.BlockSpec((step, rows), lambda i: (i, 0)),
        out_shape=jax.ShapeDtypeStruct((cols, rows), F32),
        cost_estimate=pl.CostEstimate(flops=0, bytes_accessed=8 * rows * cols, transcendentals=0),
        compiler_params=pltpu.CompilerParams(vmem_limit_bytes=VMEM_BYTES),
        name="turn_samples",
    )(x, roots)


def lane_tile(a, n):
    return a[:, n * LANES : (n + 1) * LANES]


def coef_kernel(t_ref, w_ref, x_ref, odd_ref, o_ref, s_ref):
    table = split(t_ref[...])
    tiles = s_ref.shape[0]
    for e, part in enumerate((x_ref, odd_ref)):
        got = dot3(table, split(part[...] * w_ref[...]), NN)
        for n in range(tiles):
            s_ref.at[n][pl.ds(e, 2 * NBINS, stride=2), :] = lane_tile(got, n)
    for n in range(tiles):
        o_ref[:, n] = s_ref[n].reshape(-1, 8, LANES)


def coefs(table, roots, x, odd, first):
    rows, cols = x.shape[0], x.shape[1] - first
    step = 512
    return pl.pallas_call(
        coef_kernel,
        grid=(cols // step,),
        in_specs=[
            pl.BlockSpec((2 * NBINS, rows), lambda i: (0, 0)),
            pl.BlockSpec((1, step), lambda i: (0, first // step + i)),
            pl.BlockSpec((rows, step), lambda i: (0, first // step + i)),
            pl.BlockSpec((rows, step), lambda i: (0, i)),
        ],
        out_specs=pl.BlockSpec((NBINS // 2, step // LANES, 8, LANES), lambda i: (0, i, 0, 0)),
        out_shape=jax.ShapeDtypeStruct((NBINS // 2, cols // LANES, 8, LANES), F32),
        scratch_shapes=[pltpu.VMEM((step // LANES, 4 * NBINS, LANES), F32)],
        cost_estimate=pl.CostEstimate(
            flops=12 * 2 * NBINS * rows * cols, bytes_accessed=10 * rows * cols, transcendentals=0
        ),
        compiler_params=pltpu.CompilerParams(vmem_limit_bytes=VMEM_BYTES),
        name="coefs_by_bin",
    )(table, roots, x, odd)


def re_im(gram):
    half = gram.shape[0] // 2
    other = pltpu.roll(gram[half:], half, 1)
    lane = lax.broadcasted_iota(jnp.int32, other.shape, 1)
    return gram[:half] + jnp.where(lane < half, other, -other)


def diagonal(out):
    row = lax.broadcasted_iota(jnp.int32, out.shape, 0)
    lane = lax.broadcasted_iota(jnp.int32, out.shape, 1)
    return jnp.sum(jnp.where(row == lane, out, 0.0), axis=0, keepdims=True)


def two_traces(first, second):
    return diagonal(first) + pltpu.roll(diagonal(second), BLOCKS, 1)


def points_kernel(where_ref, t_ref, x_ref, c_ref, o_ref, s_ref):
    tm_count, pts = x_ref.shape[0], x_ref.shape[1]
    tiles = s_ref.shape[0]
    table = split(t_ref[...])
    blank = jnp.zeros((tiles * LANES - pts, NFFT), F32)

    def transform(j, samples):
        got = dot3(table, split(jnp.concatenate([samples, blank], axis=0)), NT)
        for n in range(tiles):
            s_ref.at[n][pl.ds(j, 2 * NBINS, stride=BLOCKS), :] = lane_tile(got, n)

    def both(t, following):
        x = x_ref[t]
        transform(2 * t, x)
        transform(2 * t + 1, jnp.concatenate([x[:, HOP:], following], axis=1))

    def four(i, carry):
        for n in range(4):
            both(4 * i + n, x_ref[4 * i + n + 1][:, :HOP])
        return carry

    lax.fori_loop(0, tm_count // 4 - 1, four, 0)
    for t in range(tm_count - 4, tm_count - 1):
        both(t, x_ref[t + 1][:, :HOP])
    both(tm_count - 1, c_ref[...])

    y, core, x_at, z_at = (where_ref[n] for n in range(4))

    def owner(t):
        xr = lax.rem(t // 8 - x_at + 4, 4)
        z = lax.rem(t, 8)
        zr = lax.rem(z - z_at + 8, 8)
        outs = []
        for b in range(2):
            mine = pl.ds(pl.multiple_of(2 * BLOCKS * (2 * t + b), 2 * BLOCKS), 2 * BLOCKS)
            rows = split(jnp.concatenate([s_ref[n, mine] for n in range(tiles)], axis=1))
            outs.append(re_im(dot3(rows, rows, NT)))
        traces = two_traces(*outs)
        for s in range(8):
            cr = lax.rem(s % 2 + core, 2)
            yr = lax.rem(s // 2 - y + 4, 4)
            for b in range(2):
                o_ref[cr, yr, xr, 2 * zr + b] = outs[b][8 * s : 8 * s + 8]
            o_ref[cr, yr, xr, 16, pl.ds(z, 1), :] = traces

    def four_owners(i, carry):
        for n in range(4):
            owner(4 * i + n)
        return carry

    lax.fori_loop(0, tm_count // 4, four_owners, 0)


def points_gram(where, table, samples, closing):
    wide = -(-samples.shape[1] // NFFT) * NFFT
    vmem = pl.BlockSpec(memory_space=pltpu.VMEM)
    return pl.pallas_call(
        points_kernel,
        in_specs=[pl.BlockSpec(memory_space=pltpu.SMEM), vmem, vmem, vmem],
        out_specs=vmem,
        out_shape=jax.ShapeDtypeStruct((2, 4, 4, 17, 8, LANES), F32),
        scratch_shapes=[pltpu.VMEM((wide // LANES, 2 * NBINS * BLOCKS, LANES), F32)],
        cost_estimate=pl.CostEstimate(
            flops=6 * 10**9, bytes_accessed=20 * 10**6, transcendentals=0
        ),
        compiler_params=pltpu.CompilerParams(vmem_limit_bytes=VMEM_BYTES),
        name="points_gram",
    )(where, table, samples, closing)


def bins_kernel(a_ref, o_ref, s_ref):
    tiles = s_ref.shape[0]
    tm_count = a_ref.shape[0] // (8 * tiles)
    for n in range(tiles):
        for c in range(4):
            for e in range(2):
                got = a_ref[pl.ds(8 * n + 2 * c + e, tm_count, stride=8 * tiles), :]
                if e == 1 and n >= tiles // 2:
                    got = pltpu.roll(got, tm_count - 1, 0)
                s_ref.at[n][pl.ds(c * BLOCKS + e, tm_count, stride=2), :] = got
    outs = []
    for b in range(2):
        mine = pl.ds(2 * BLOCKS * b, 2 * BLOCKS)
        rows = split(jnp.concatenate([s_ref[n, mine] for n in range(tiles)], axis=1))
        outs.append(re_im(dot3(rows, rows, NT)))
    traces = jnp.broadcast_to(two_traces(*outs), (8, LANES))
    for s in range(8):
        for b in range(2):
            o_ref[s, b] = outs[b][8 * s : 8 * s + 8]
        o_ref[s, 2] = traces


def bins_gram(coef):
    vmem = pl.BlockSpec(memory_space=pltpu.VMEM)
    tiles = coef.shape[1]
    return pl.pallas_call(
        bins_kernel,
        in_specs=[vmem],
        out_specs=vmem,
        out_shape=jax.ShapeDtypeStruct((8, 3, 8, LANES), F32),
        scratch_shapes=[pltpu.VMEM((tiles, 4 * BLOCKS, LANES), F32)],
        cost_estimate=pl.CostEstimate(
            flops=5 * 10**8, bytes_accessed=2 * 10**6, transcendentals=0
        ),
        compiler_params=pltpu.CompilerParams(vmem_limit_bytes=VMEM_BYTES),
        name="bins_gram",
    )(coef.reshape(-1, LANES))


def norm_kernel(where_ref, r_ref, *refs):
    o_ref = refs[-1]
    total = r_ref[0]
    for s in range(1, 8):
        total = total + r_ref[s]
    for ref in refs[:-1]:
        total = total + ref[...]
    row = lax.broadcasted_iota(jnp.int32, (8, LANES), 0)
    lane = lax.broadcasted_iota(jnp.int32, (8, LANES), 1)
    for b in range(2):
        mine = (row == where_ref[3]) & (lane // BLOCKS == b)
        energy = jnp.sum(jnp.where(mine, total[2], 0.0), keepdims=True)
        out = total[b] * (BLOCKS / energy)
        o_ref[b, 0] = out[:, :BLOCKS]
        o_ref[b, 1] = out[:, BLOCKS:]


def normalized(where, parts, others):
    vmem = pl.BlockSpec(memory_space=pltpu.VMEM)
    return pl.pallas_call(
        norm_kernel,
        in_specs=[pl.BlockSpec(memory_space=pltpu.SMEM)] + [vmem] * (1 + len(others)),
        out_specs=vmem,
        out_shape=jax.ShapeDtypeStruct((2, 2, 8, BLOCKS), F32),
        name="normalize",
    )(where, parts, *others)


def by_y(d):
    return [(2 * y + c, 2 * ((y + d) % 4) + c) for y in range(4) for c in range(2)]


def by_x(d):
    return [(8 * x + z, 8 * ((x + d) % 4) + z) for x in range(4) for z in range(8)]


def by_z(d):
    return [(8 * x + z, 8 * x + (z + d) % 8) for x in range(4) for z in range(8)]


def summed_up(held, axis, steps, pairs):
    return sum([lax.ppermute(held[d], axis, pairs(d)) for d in range(1, steps)], held[0])


def odd_blocks(snapshots, closing, tm, tm_count, first):
    middle = (first + snapshots.shape[1]) // 2
    down = lax.ppermute(
        snapshots[:HOP, first:middle], "tm", [(t, t - 1) for t in range(1, tm_count)]
    )
    up = lax.ppermute(
        snapshots[HOP:, middle:], "tm", [(t, (t + 1) % tm_count) for t in range(tm_count)]
    )

    def finish(down, up):
        after = jnp.where(tm == tm_count - 1, closing[:, first:middle], down)
        ending = jnp.where(tm == 0, closing[:, middle:], snapshots[:HOP, middle:])
        return jnp.concatenate(
            [
                jnp.concatenate([snapshots[HOP:, first:middle], after], axis=0),
                jnp.concatenate([up, ending], axis=0),
            ],
            axis=1,
        )

    return down, up, finish


def body(snapshots, closing, weights, bin_index):
    tm_count = lax.axis_size("tm")
    tm, space = lax.axis_index("tm"), lax.axis_index("space")
    where = jnp.stack([space // 2, space % 2, tm // 8, tm % 8]).astype(jnp.int32)
    first = tm_count * PTS_TM
    roots = jnp.sqrt(weights)[None, :]
    down, up, finish = odd_blocks(snapshots, closing, tm, tm_count, first)
    sent = turned(snapshots, roots, first).reshape(tm_count, PTS_TM, NFFT)
    sent, down, up = lax.optimization_barrier((sent, down, up))
    samples = lax.all_to_all(sent, "tm", 0, 0, tiled=True)
    table = table_rows(bin_index, NFFT)
    coef = coefs(table, roots, snapshots, finish(down, up), first)
    own_roots = lax.dynamic_slice(roots, (0, tm * PTS_TM), (1, PTS_TM))
    own_closing = lax.dynamic_slice(closing, (0, tm * PTS_TM), (HOP, PTS_TM)) * own_roots
    samples, coef, own_closing = lax.optimization_barrier((samples, coef, own_closing.T))
    by_bin = lax.all_to_all(coef, "tm", 0, 0, tiled=True)
    parts = points_gram(where, table, samples, own_closing)
    held = parts[0] + lax.ppermute(parts[1], "space", [(s, s ^ 1) for s in range(8)])
    held = summed_up(summed_up(held, "space", 4, by_y), "tm", 4, by_x)
    by_bin, held = lax.optimization_barrier((by_bin, held))
    others = [jnp.concatenate([held[2 * d : 2 * d + 2], held[16:]], axis=0) for d in range(8)]
    others[1:] = [lax.ppermute(others[d], "tm", by_z(d)) for d in range(1, 8)]
    parts = lax.all_to_all(bins_gram(by_bin), "space", 0, 0, tiled=True)
    return normalized(where, parts, others)


def solution(mesh):
    return jax.shard_map(
        body,
        mesh=mesh,
        in_specs=(P("tm", "space"), P(None, "space"), P("space"), P()),
        out_specs=P("tm", None, "space", None),
        check_vma=False,
    )
```

```python
import jax
import jax.numpy as jnp
from jax import lax
from jax.experimental import pallas as pl
from jax.experimental.pallas import tpu as pltpu
from jax.sharding import PartitionSpec as P

NFFT = 256
NBINS = 64
HOP = NFFT // 2
BLOCKS = 64
LANES = 128
PTS_TM = 176
F32, BF16 = jnp.float32, jnp.bfloat16
VMEM_BYTES = 50 * 2**20


def split(a):
    hi = a.astype(BF16)
    return hi, (a - hi.astype(F32)).astype(BF16)


def dot3(a, b, dims):
    dg = lambda u, v: lax.dot_general(u, v, (dims, ((), ())), preferred_element_type=F32)
    return dg(a[0], b[0]) + dg(a[0], b[1]) + dg(a[1], b[0])


NN, NT = ((1,), (0,)), ((1,), (1,))


def table_rows(bin_index, length):
    sample = jnp.arange(length, dtype=jnp.int32)
    window = 0.5 - 0.5 * jnp.cos(2.0 * jnp.pi * sample.astype(F32) / length)
    turns = sample[None, :] * bin_index[:, None] % length
    angle = 2.0 * jnp.pi * turns.astype(F32) / length
    paired = jnp.stack([window * jnp.cos(angle), -window * jnp.sin(angle)], axis=1)
    return paired.reshape(2 * bin_index.shape[0], length)


def turn_kernel(x_ref, w_ref, o_ref):
    o_ref[...] = (x_ref[...] * w_ref[...]).T


def turned(x, roots, cols):
    rows, step = x.shape[0], 512
    return pl.pallas_call(
        turn_kernel,
        grid=(cols // step,),
        in_specs=[
            pl.BlockSpec((rows, step), lambda i: (0, i)),
            pl.BlockSpec((1, step), lambda i: (0, i)),
        ],
        out_specs=pl.BlockSpec((step, rows), lambda i: (i, 0)),
        out_shape=jax.ShapeDtypeStruct((cols, rows), F32),
        cost_estimate=pl.CostEstimate(flops=0, bytes_accessed=8 * rows * cols, transcendentals=0),
        compiler_params=pltpu.CompilerParams(vmem_limit_bytes=VMEM_BYTES),
        name="turn_samples",
    )(x, roots)


def lane_tile(a, n):
    return a[:, n * LANES : (n + 1) * LANES]


def coef_kernel(t_ref, w_ref, x_ref, odd_ref, o_ref, s_ref):
    table = split(t_ref[...])
    tiles = s_ref.shape[0]
    for e, part in enumerate((x_ref, odd_ref)):
        got = dot3(table, split(part[...] * w_ref[...]), NN)
        for n in range(tiles):
            s_ref.at[n][pl.ds(e, 2 * NBINS, stride=2), :] = lane_tile(got, n)
    for n in range(tiles):
        o_ref[:, n] = s_ref[n].reshape(-1, 8, LANES)


def coefs(table, roots, x, odd, first):
    rows, cols = x.shape[0], x.shape[1] - first
    step = 512
    return pl.pallas_call(
        coef_kernel,
        grid=(cols // step,),
        in_specs=[
            pl.BlockSpec((2 * NBINS, rows), lambda i: (0, 0)),
            pl.BlockSpec((1, step), lambda i: (0, first // step + i)),
            pl.BlockSpec((rows, step), lambda i: (0, first // step + i)),
            pl.BlockSpec((rows, step), lambda i: (0, i)),
        ],
        out_specs=pl.BlockSpec((NBINS // 2, step // LANES, 8, LANES), lambda i: (0, i, 0, 0)),
        out_shape=jax.ShapeDtypeStruct((NBINS // 2, cols // LANES, 8, LANES), F32),
        scratch_shapes=[pltpu.VMEM((step // LANES, 4 * NBINS, LANES), F32)],
        cost_estimate=pl.CostEstimate(
            flops=12 * 2 * NBINS * rows * cols, bytes_accessed=10 * rows * cols, transcendentals=0
        ),
        compiler_params=pltpu.CompilerParams(vmem_limit_bytes=VMEM_BYTES),
        name="coefs_by_bin",
    )(table, roots, x, odd)


def re_im(gram):
    half = gram.shape[0] // 2
    other = pltpu.roll(gram[half:], half, 1)
    lane = lax.broadcasted_iota(jnp.int32, other.shape, 1)
    return gram[:half] + jnp.where(lane < half, other, -other)


def iotas(shape):
    return (lax.broadcasted_iota(jnp.int32, shape, 0), lax.broadcasted_iota(jnp.int32, shape, 1))


def swapped(out):
    return pltpu.roll(out, BLOCKS, 1)


def packed(first, second):
    row, lane = iotas(first.shape)
    lower = lane % BLOCKS < row
    return jnp.where(
        lane < BLOCKS,
        jnp.where(lower, swapped(first), first),
        jnp.where(lower, second, swapped(second)),
    )


def unpacked(squares):
    row, lane = iotas((BLOCKS, LANES))
    column = lane % BLOCKS
    mirrored = squares.T
    outs = []
    for b in range(2):
        mirror = mirrored[BLOCKS * b : BLOCKS * (b + 1)]
        mirror = jnp.concatenate([mirror, mirror], axis=1)
        square = squares[:, BLOCKS * b : BLOCKS * (b + 1)]
        square = jnp.concatenate([square, square], axis=1)
        real = jnp.where(column >= row, square, mirror)
        imag = jnp.where(column < row, square, jnp.where(column > row, -mirror, 0.0))
        outs.append(jnp.where(lane < BLOCKS, real, imag))
    return outs


def points_kernel(where_ref, t_ref, x_ref, c_ref, o_ref, s_ref):
    tm_count, pts = x_ref.shape[0], x_ref.shape[1]
    tiles = s_ref.shape[0]
    table = split(t_ref[...])
    blank = jnp.zeros((tiles * LANES - pts, NFFT), F32)

    def transform(j, samples):
        got = dot3(table, split(jnp.concatenate([samples, blank], axis=0)), NT)
        for n in range(tiles):
            s_ref.at[n][pl.ds(j, 2 * NBINS, stride=BLOCKS), :] = lane_tile(got, n)

    def both(t, following):
        x = x_ref[t]
        transform(2 * t, x)
        transform(2 * t + 1, jnp.concatenate([x[:, HOP:], following], axis=1))

    def four(i, carry):
        for n in range(4):
            both(4 * i + n, x_ref[4 * i + n + 1][:, :HOP])
        return carry

    lax.fori_loop(0, tm_count // 4 - 1, four, 0)
    for t in range(tm_count - 4, tm_count - 1):
        both(t, x_ref[t + 1][:, :HOP])
    both(tm_count - 1, c_ref[...])

    x_at, z_at = where_ref[0], where_ref[1]

    def owner(t):
        xr = lax.rem(t // 8 - x_at + 4, 4)
        zr = lax.rem(lax.rem(t, 8) - z_at + 8, 8)
        outs = []
        for b in range(2):
            mine = pl.ds(pl.multiple_of(2 * BLOCKS * (2 * t + b), 2 * BLOCKS), 2 * BLOCKS)
            rows = split(jnp.concatenate([s_ref[n, mine] for n in range(tiles)], axis=1))
            outs.append(re_im(dot3(rows, rows, NT)))
        o_ref[xr, zr] = packed(*outs)

    def four_owners(i, carry):
        for n in range(4):
            owner(4 * i + n)
        return carry

    lax.fori_loop(0, tm_count // 4, four_owners, 0)


def points_gram(where, table, samples, closing):
    wide = -(-samples.shape[1] // NFFT) * NFFT
    vmem = pl.BlockSpec(memory_space=pltpu.VMEM)
    return pl.pallas_call(
        points_kernel,
        in_specs=[pl.BlockSpec(memory_space=pltpu.SMEM), vmem, vmem, vmem],
        out_specs=vmem,
        out_shape=jax.ShapeDtypeStruct((4, 8, BLOCKS, LANES), F32),
        scratch_shapes=[pltpu.VMEM((wide // LANES, 2 * NBINS * BLOCKS, LANES), F32)],
        cost_estimate=pl.CostEstimate(
            flops=6 * 10**9, bytes_accessed=20 * 10**6, transcendentals=0
        ),
        compiler_params=pltpu.CompilerParams(vmem_limit_bytes=VMEM_BYTES),
        name="points_gram",
    )(where, table, samples, closing)


def bins_kernel(a_ref, *refs):
    o_ref, s_ref = refs[-2:]
    tiles = s_ref.shape[0]
    tm_count = a_ref.shape[0] // (8 * tiles)
    for n in range(tiles):
        for c in range(4):
            for e in range(2):
                got = a_ref[pl.ds(8 * n + 2 * c + e, tm_count, stride=8 * tiles), :]
                if e == 1 and n >= tiles // 2:
                    got = pltpu.roll(got, tm_count - 1, 0)
                s_ref.at[n][pl.ds(c * BLOCKS + e, tm_count, stride=2), :] = got
    outs = unpacked(sum([ref[...] for ref in refs[1:-2]], refs[0][...]))
    row, lane = iotas((BLOCKS, LANES))
    for b in range(2):
        mine = pl.ds(2 * BLOCKS * b, 2 * BLOCKS)
        rows = split(jnp.concatenate([s_ref[n, mine] for n in range(tiles)], axis=1))
        outs[b] = outs[b] + re_im(dot3(rows, rows, NT))
    traces = [jnp.sum(jnp.where(row == lane, out, 0.0), keepdims=True) for out in outs]
    traces = jnp.where(row[:8] == 0, traces[0], traces[1])
    for s in range(8):
        for b in range(2):
            o_ref[s, b] = outs[b][8 * s : 8 * s + 8]
        o_ref[s, 2] = traces


def bins_gram(coef, others):
    vmem = pl.BlockSpec(memory_space=pltpu.VMEM)
    tiles = coef.shape[1]
    return pl.pallas_call(
        bins_kernel,
        in_specs=[vmem] * (1 + len(others)),
        out_specs=vmem,
        out_shape=jax.ShapeDtypeStruct((8, 3, 8, LANES), F32),
        scratch_shapes=[pltpu.VMEM((tiles, 4 * BLOCKS, LANES), F32)],
        cost_estimate=pl.CostEstimate(
            flops=5 * 10**8, bytes_accessed=2 * 10**6, transcendentals=0
        ),
        compiler_params=pltpu.CompilerParams(vmem_limit_bytes=VMEM_BYTES),
        name="bins_gram",
    )(coef.reshape(-1, LANES), *others)


def norm_kernel(r_ref, o_ref):
    total = r_ref[0]
    for s in range(1, 8):
        total = total + r_ref[s]
    for b in range(2):
        out = total[b] * (BLOCKS / total[2, b : b + 1])
        o_ref[b, 0] = out[:, :BLOCKS]
        o_ref[b, 1] = out[:, BLOCKS:]


def normalized(parts):
    vmem = pl.BlockSpec(memory_space=pltpu.VMEM)
    return pl.pallas_call(
        norm_kernel,
        in_specs=[vmem],
        out_specs=vmem,
        out_shape=jax.ShapeDtypeStruct((2, 2, 8, BLOCKS), F32),
        name="normalize",
    )(parts)


def by_x(d):
    return [(8 * x + z, 8 * ((x + d) % 4) + z) for x in range(4) for z in range(8)]


def by_z(d):
    return [(8 * x + z, 8 * x + (z + d) % 8) for x in range(4) for z in range(8)]


def sent_on(held, steps, pairs):
    return [held[0]] + [lax.ppermute(held[d], "tm", pairs(d)) for d in range(1, steps)]


def odd_blocks(snapshots, closing, tm, tm_count, first):
    middle = (first + snapshots.shape[1]) // 2
    down = lax.ppermute(
        snapshots[:HOP, first:middle], "tm", [(t, t - 1) for t in range(1, tm_count)]
    )
    up = lax.ppermute(
        snapshots[HOP:, middle:], "tm", [(t, (t + 1) % tm_count) for t in range(tm_count)]
    )

    def finish(down, up):
        after = jnp.where(tm == tm_count - 1, closing[:, first:middle], down)
        ending = jnp.where(tm == 0, closing[:, middle:], snapshots[:HOP, middle:])
        return jnp.concatenate(
            [
                jnp.concatenate([snapshots[HOP:, first:middle], after], axis=0),
                jnp.concatenate([up, ending], axis=0),
            ],
            axis=1,
        )

    return down, up, finish


def body(snapshots, closing, weights, bin_index):
    tm_count = lax.axis_size("tm")
    tm = lax.axis_index("tm")
    where = jnp.stack([tm // 8, tm % 8]).astype(jnp.int32)
    first = tm_count * PTS_TM
    roots = jnp.sqrt(weights)[None, :]
    down, up, finish = odd_blocks(snapshots, closing, tm, tm_count, first)
    sent = turned(snapshots, roots, first).reshape(tm_count, PTS_TM, NFFT)
    sent, down, up = lax.optimization_barrier((sent, down, up))
    samples = lax.all_to_all(sent, "tm", 0, 0, tiled=True)
    table = table_rows(bin_index, NFFT)
    coef = coefs(table, roots, snapshots, finish(down, up), first)
    own_roots = lax.dynamic_slice(roots, (0, tm * PTS_TM), (1, PTS_TM))
    own_closing = lax.dynamic_slice(closing, (0, tm * PTS_TM), (HOP, PTS_TM)) * own_roots
    samples, coef, own_closing = lax.optimization_barrier((samples, coef, own_closing.T))
    by_bin = lax.all_to_all(coef, "tm", 0, 0, tiled=True)
    parts = points_gram(where, table, samples, own_closing)
    others = sent_on(sum(sent_on(parts, 4, by_x)), 8, by_z)
    parts = lax.all_to_all(bins_gram(by_bin, others), "space", 0, 0, tiled=True)
    return normalized(parts)


def solution(mesh):
    return jax.shard_map(
        body,
        mesh=mesh,
        in_specs=(P("tm", "space"), P(None, "space"), P("space"), P()),
        out_specs=P("tm", None, "space", None),
        check_vma=False,
    )
```

```python
import math

import jax
import jax.numpy as jnp
from jax import lax
from jax.experimental import pallas as pl
from jax.experimental.pallas import tpu as pltpu
from jax.sharding import PartitionSpec as P

NFFT = 256
NBINS = 64
HOP = NFFT // 2
BLOCKS = 64
LANES = 128
PTS_TM = 152
F32, BF16 = jnp.float32, jnp.bfloat16
VMEM_BYTES = 50 * 2**20


def split(a):
    hi = a.astype(BF16)
    return hi, (a - hi.astype(F32)).astype(BF16)


def dot3(a, b, dims):
    dg = lambda u, v: lax.dot_general(u, v, (dims, ((), ())), preferred_element_type=F32)
    return dg(a[0], b[0]) + dg(a[0], b[1]) + dg(a[1], b[0])


NN, NT = ((1,), (0,)), ((1,), (1,))


def table_rows(bin_index, length):
    sample = jnp.arange(length, dtype=jnp.int32)
    window = 0.5 - 0.5 * jnp.cos(2.0 * jnp.pi * sample.astype(F32) / length)
    turns = sample[None, :] * bin_index[:, None] % length
    angle = 2.0 * jnp.pi * turns.astype(F32) / length
    paired = jnp.stack([window * jnp.cos(angle), -window * jnp.sin(angle)], axis=1)
    return paired.reshape(2 * bin_index.shape[0], length)


def widest(cols):
    return max(n * LANES for n in range(1, 7) if cols % (n * LANES) == 0)


def turn_kernel(x_ref, w_ref, o_ref):
    o_ref[...] = (x_ref[...] * w_ref[...]).T


def turned(x, roots, cols):
    rows, step = x.shape[0], widest(cols)
    return pl.pallas_call(
        turn_kernel,
        grid=(cols // step,),
        in_specs=[
            pl.BlockSpec((rows, step), lambda i: (0, i)),
            pl.BlockSpec((1, step), lambda i: (0, i)),
        ],
        out_specs=pl.BlockSpec((step, rows), lambda i: (i, 0)),
        out_shape=jax.ShapeDtypeStruct((cols, rows), F32),
        cost_estimate=pl.CostEstimate(flops=0, bytes_accessed=8 * rows * cols, transcendentals=0),
        compiler_params=pltpu.CompilerParams(vmem_limit_bytes=VMEM_BYTES),
        name="turn_samples",
    )(x, roots)


def lane_tile(a, n):
    return a[:, n * LANES : (n + 1) * LANES]


def coef_kernel(t_ref, w_ref, x_ref, odd_ref, o_ref, s_ref):
    table = split(t_ref[...])
    tiles = s_ref.shape[0]
    for e, part in enumerate((x_ref, odd_ref)):
        got = dot3(table, split(part[...] * w_ref[...]), NN)
        for n in range(tiles):
            s_ref.at[n][pl.ds(e, 2 * NBINS, stride=2), :] = lane_tile(got, n)
    for n in range(tiles):
        o_ref[:, n] = s_ref[n].reshape(-1, 8, LANES)


def coefs(table, roots, x, odd, first):
    rows, cols = x.shape[0], x.shape[1] - first
    step = widest(math.gcd(first, cols))
    return pl.pallas_call(
        coef_kernel,
        grid=(cols // step,),
        in_specs=[
            pl.BlockSpec((2 * NBINS, rows), lambda i: (0, 0)),
            pl.BlockSpec((1, step), lambda i: (0, first // step + i)),
            pl.BlockSpec((rows, step), lambda i: (0, first // step + i)),
            pl.BlockSpec((rows, step), lambda i: (0, i)),
        ],
        out_specs=pl.BlockSpec((NBINS // 2, step // LANES, 8, LANES), lambda i: (0, i, 0, 0)),
        out_shape=jax.ShapeDtypeStruct((NBINS // 2, cols // LANES, 8, LANES), F32),
        scratch_shapes=[pltpu.VMEM((step // LANES, 4 * NBINS, LANES), F32)],
        cost_estimate=pl.CostEstimate(
            flops=12 * 2 * NBINS * rows * cols, bytes_accessed=10 * rows * cols, transcendentals=0
        ),
        compiler_params=pltpu.CompilerParams(vmem_limit_bytes=VMEM_BYTES),
        name="coefs_by_bin",
    )(table, roots, x, odd)


def re_im(gram):
    half = gram.shape[0] // 2
    other = pltpu.roll(gram[half:], half, 1)
    lane = lax.broadcasted_iota(jnp.int32, other.shape, 1)
    return gram[:half] + jnp.where(lane < half, other, -other)


def iotas(shape):
    return (lax.broadcasted_iota(jnp.int32, shape, 0), lax.broadcasted_iota(jnp.int32, shape, 1))


def swapped(out):
    return pltpu.roll(out, BLOCKS, 1)


def packed(first, second):
    row, lane = iotas(first.shape)
    lower = lane % BLOCKS < row
    return jnp.where(
        lane < BLOCKS,
        jnp.where(lower, swapped(first), first),
        jnp.where(lower, second, swapped(second)),
    )


def unpacked(squares):
    row, lane = iotas((BLOCKS, LANES))
    column = lane % BLOCKS
    mirrored = squares.T
    outs = []
    for b in range(2):
        mirror = mirrored[BLOCKS * b : BLOCKS * (b + 1)]
        mirror = jnp.concatenate([mirror, mirror], axis=1)
        square = squares[:, BLOCKS * b : BLOCKS * (b + 1)]
        square = jnp.concatenate([square, square], axis=1)
        real = jnp.where(column >= row, square, mirror)
        imag = jnp.where(column < row, square, jnp.where(column > row, -mirror, 0.0))
        outs.append(jnp.where(lane < BLOCKS, real, imag))
    return outs


def points_kernel(where_ref, t_ref, x_ref, c_ref, o_ref, s_ref):
    tm_count, pts = x_ref.shape[0], x_ref.shape[1]
    tiles = s_ref.shape[0]
    table = split(t_ref[...])
    blank = jnp.zeros((tiles * LANES - pts, NFFT), F32)

    def transform(j, samples):
        got = dot3(table, split(jnp.concatenate([samples, blank], axis=0)), NT)
        for n in range(tiles):
            s_ref.at[n][pl.ds(j, 2 * NBINS, stride=BLOCKS), :] = lane_tile(got, n)

    def both(t, following):
        x = x_ref[t]
        transform(2 * t, x)
        transform(2 * t + 1, jnp.concatenate([x[:, HOP:], following], axis=1))

    def four(i, carry):
        for n in range(4):
            both(4 * i + n, x_ref[4 * i + n + 1][:, :HOP])
        return carry

    lax.fori_loop(0, tm_count // 4 - 1, four, 0)
    for t in range(tm_count - 4, tm_count - 1):
        both(t, x_ref[t + 1][:, :HOP])
    both(tm_count - 1, c_ref[...])

    x_at, z_at = where_ref[0], where_ref[1]

    def owner(t):
        xr = lax.rem(t // 8 - x_at + 4, 4)
        zr = lax.rem(lax.rem(t, 8) - z_at + 8, 8)
        outs = []
        for b in range(2):
            mine = pl.ds(pl.multiple_of(2 * BLOCKS * (2 * t + b), 2 * BLOCKS), 2 * BLOCKS)
            rows = split(jnp.concatenate([s_ref[n, mine] for n in range(tiles)], axis=1))
            outs.append(re_im(dot3(rows, rows, NT)))
        o_ref[xr, zr] = packed(*outs)

    def four_owners(i, carry):
        for n in range(4):
            owner(4 * i + n)
        return carry

    lax.fori_loop(0, tm_count // 4, four_owners, 0)


def points_gram(where, table, samples, closing):
    wide = -(-samples.shape[1] // NFFT) * NFFT
    vmem = pl.BlockSpec(memory_space=pltpu.VMEM)
    return pl.pallas_call(
        points_kernel,
        in_specs=[pl.BlockSpec(memory_space=pltpu.SMEM), vmem, vmem, vmem],
        out_specs=vmem,
        out_shape=jax.ShapeDtypeStruct((4, 8, BLOCKS, LANES), F32),
        scratch_shapes=[pltpu.VMEM((wide // LANES, 2 * NBINS * BLOCKS, LANES), F32)],
        cost_estimate=pl.CostEstimate(
            flops=6 * 10**9, bytes_accessed=20 * 10**6, transcendentals=0
        ),
        compiler_params=pltpu.CompilerParams(vmem_limit_bytes=VMEM_BYTES),
        name="points_gram",
    )(where, table, samples, closing)


def bins_kernel(a_ref, *refs):
    o_ref, s_ref = refs[-2:]
    tiles = s_ref.shape[0]
    tm_count = a_ref.shape[0] // (8 * tiles)
    for n in range(tiles):
        for c in range(4):
            for e in range(2):
                got = a_ref[pl.ds(8 * n + 2 * c + e, tm_count, stride=8 * tiles), :]
                if e == 1 and n >= tiles // 2:
                    got = pltpu.roll(got, tm_count - 1, 0)
                s_ref.at[n][pl.ds(c * BLOCKS + e, tm_count, stride=2), :] = got
    outs = unpacked(sum([ref[...] for ref in refs[1:-2]], refs[0][...]))
    row, lane = iotas((BLOCKS, LANES))
    for b in range(2):
        mine = pl.ds(2 * BLOCKS * b, 2 * BLOCKS)
        rows = split(jnp.concatenate([s_ref[n, mine] for n in range(tiles)], axis=1))
        outs[b] = outs[b] + re_im(dot3(rows, rows, NT))
    traces = [jnp.sum(jnp.where(row == lane, out, 0.0), keepdims=True) for out in outs]
    traces = jnp.where(row[:8] == 0, traces[0], traces[1])
    for s in range(8):
        for b in range(2):
            o_ref[s, b] = outs[b][8 * s : 8 * s + 8]
        o_ref[s, 2] = traces


def bins_gram(coef, others):
    vmem = pl.BlockSpec(memory_space=pltpu.VMEM)
    tiles = coef.shape[1]
    return pl.pallas_call(
        bins_kernel,
        in_specs=[vmem] * (1 + len(others)),
        out_specs=vmem,
        out_shape=jax.ShapeDtypeStruct((8, 3, 8, LANES), F32),
        scratch_shapes=[pltpu.VMEM((tiles, 4 * BLOCKS, LANES), F32)],
        cost_estimate=pl.CostEstimate(
            flops=5 * 10**8, bytes_accessed=2 * 10**6, transcendentals=0
        ),
        compiler_params=pltpu.CompilerParams(vmem_limit_bytes=VMEM_BYTES),
        name="bins_gram",
    )(coef.reshape(-1, LANES), *others)


def norm_kernel(r_ref, o_ref):
    total = r_ref[0]
    for s in range(1, 8):
        total = total + r_ref[s]
    for b in range(2):
        out = total[b] * (BLOCKS / total[2, b : b + 1])
        o_ref[b, 0] = out[:, :BLOCKS]
        o_ref[b, 1] = out[:, BLOCKS:]


def normalized(parts):
    vmem = pl.BlockSpec(memory_space=pltpu.VMEM)
    return pl.pallas_call(
        norm_kernel,
        in_specs=[vmem],
        out_specs=vmem,
        out_shape=jax.ShapeDtypeStruct((2, 2, 8, BLOCKS), F32),
        name="normalize",
    )(parts)


def by_x(d):
    return [(8 * x + z, 8 * ((x + d) % 4) + z) for x in range(4) for z in range(8)]


def by_z(d):
    return [(8 * x + z, 8 * x + (z + d) % 8) for x in range(4) for z in range(8)]


def sent_on(held, steps, pairs):
    return [held[0]] + [lax.ppermute(held[d], "tm", pairs(d)) for d in range(1, steps)]


def odd_blocks(snapshots, closing, tm, tm_count, first):
    middle = (first + snapshots.shape[1]) // 2
    down = lax.ppermute(
        snapshots[:HOP, first:middle], "tm", [(t, t - 1) for t in range(1, tm_count)]
    )
    up = lax.ppermute(
        snapshots[HOP:, middle:], "tm", [(t, (t + 1) % tm_count) for t in range(tm_count)]
    )

    def finish(down, up):
        after = jnp.where(tm == tm_count - 1, closing[:, first:middle], down)
        ending = jnp.where(tm == 0, closing[:, middle:], snapshots[:HOP, middle:])
        return jnp.concatenate(
            [
                jnp.concatenate([snapshots[HOP:, first:middle], after], axis=0),
                jnp.concatenate([up, ending], axis=0),
            ],
            axis=1,
        )

    return down, up, finish


def body(snapshots, closing, weights, bin_index):
    tm_count = lax.axis_size("tm")
    tm = lax.axis_index("tm")
    where = jnp.stack([tm // 8, tm % 8]).astype(jnp.int32)
    first = tm_count * PTS_TM
    roots = jnp.sqrt(weights)[None, :]
    down, up, finish = odd_blocks(snapshots, closing, tm, tm_count, first)
    sent = turned(snapshots, roots, first).reshape(tm_count, PTS_TM, NFFT)
    sent, down, up = lax.optimization_barrier((sent, down, up))
    samples = lax.all_to_all(sent, "tm", 0, 0, tiled=True)
    table = table_rows(bin_index, NFFT)
    coef = coefs(table, roots, snapshots, finish(down, up), first)
    own_roots = lax.dynamic_slice(roots, (0, tm * PTS_TM), (1, PTS_TM))
    own_closing = lax.dynamic_slice(closing, (0, tm * PTS_TM), (HOP, PTS_TM)) * own_roots
    samples, coef, own_closing = lax.optimization_barrier((samples, coef, own_closing.T))
    by_bin = lax.all_to_all(coef, "tm", 0, 0, tiled=True)
    parts = points_gram(where, table, samples, own_closing)
    others = sent_on(sum(sent_on(parts, 4, by_x)), 8, by_z)
    parts = lax.all_to_all(bins_gram(by_bin, others), "space", 0, 0, tiled=True)
    return normalized(parts)


def solution(mesh):
    return jax.shard_map(
        body,
        mesh=mesh,
        in_specs=(P("tm", "space"), P(None, "space"), P("space"), P()),
        out_specs=P("tm", None, "space", None),
        check_vma=False,
    )
```

```python
import math

import jax
import jax.numpy as jnp
from jax import lax
from jax.experimental import pallas as pl
from jax.experimental.pallas import tpu as pltpu
from jax.sharding import PartitionSpec as P

NFFT = 256
NBINS = 64
HOP = NFFT // 2
BLOCKS = 64
LANES = 128
PTS_TM = 168
F32, BF16 = jnp.float32, jnp.bfloat16
VMEM_BYTES = 50 * 2**20


def split(a):
    hi = a.astype(BF16)
    return hi, (a - hi.astype(F32)).astype(BF16)


def dot3(a, b, dims):
    dg = lambda u, v: lax.dot_general(u, v, (dims, ((), ())), preferred_element_type=F32)
    return dg(a[0], b[0]) + dg(a[0], b[1]) + dg(a[1], b[0])


NN, NT = ((1,), (0,)), ((1,), (1,))


def table_rows(bin_index, length):
    sample = jnp.arange(length, dtype=jnp.int32)
    window = 0.5 - 0.5 * jnp.cos(2.0 * jnp.pi * sample.astype(F32) / length)
    turns = sample[None, :] * bin_index[:, None] % length
    angle = 2.0 * jnp.pi * turns.astype(F32) / length
    paired = jnp.stack([window * jnp.cos(angle), -window * jnp.sin(angle)], axis=1)
    return paired.reshape(2 * bin_index.shape[0], length)


def widest(cols):
    return max(n * LANES for n in range(1, 7) if cols % (n * LANES) == 0)


def turn_kernel(x_ref, w_ref, o_ref):
    o_ref[...] = (x_ref[...] * w_ref[...]).T


def turned(x, roots, cols):
    rows, step = x.shape[0], widest(cols)
    return pl.pallas_call(
        turn_kernel,
        grid=(cols // step,),
        in_specs=[
            pl.BlockSpec((rows, step), lambda i: (0, i)),
            pl.BlockSpec((1, step), lambda i: (0, i)),
        ],
        out_specs=pl.BlockSpec((step, rows), lambda i: (i, 0)),
        out_shape=jax.ShapeDtypeStruct((cols, rows), F32),
        cost_estimate=pl.CostEstimate(flops=0, bytes_accessed=8 * rows * cols, transcendentals=0),
        compiler_params=pltpu.CompilerParams(vmem_limit_bytes=VMEM_BYTES),
        name="turn_samples",
    )(x, roots)


def lane_tile(a, n):
    return a[:, n * LANES : (n + 1) * LANES]


def coef_kernel(t_ref, w_ref, x_ref, odd_ref, o_ref, s_ref):
    table = split(t_ref[...])
    tiles = s_ref.shape[0]
    for e, part in enumerate((x_ref, odd_ref)):
        got = dot3(table, split(part[...] * w_ref[...]), NN)
        for n in range(tiles):
            s_ref.at[n][pl.ds(e, 2 * NBINS, stride=2), :] = lane_tile(got, n)
    for n in range(tiles):
        o_ref[:, n] = s_ref[n].reshape(-1, 8, LANES)


def coefs(table, roots, x, odd, first):
    rows, cols = x.shape[0], x.shape[1] - first
    step = widest(math.gcd(first, cols))
    return pl.pallas_call(
        coef_kernel,
        grid=(cols // step,),
        in_specs=[
            pl.BlockSpec((2 * NBINS, rows), lambda i: (0, 0)),
            pl.BlockSpec((1, step), lambda i: (0, first // step + i)),
            pl.BlockSpec((rows, step), lambda i: (0, first // step + i)),
            pl.BlockSpec((rows, step), lambda i: (0, i)),
        ],
        out_specs=pl.BlockSpec((NBINS // 2, step // LANES, 8, LANES), lambda i: (0, i, 0, 0)),
        out_shape=jax.ShapeDtypeStruct((NBINS // 2, cols // LANES, 8, LANES), F32),
        scratch_shapes=[pltpu.VMEM((step // LANES, 4 * NBINS, LANES), F32)],
        cost_estimate=pl.CostEstimate(
            flops=12 * 2 * NBINS * rows * cols, bytes_accessed=10 * rows * cols, transcendentals=0
        ),
        compiler_params=pltpu.CompilerParams(vmem_limit_bytes=VMEM_BYTES),
        name="coefs_by_bin",
    )(table, roots, x, odd)


def re_im(gram):
    half = gram.shape[0] // 2
    other = pltpu.roll(gram[half:], half, 1)
    lane = lax.broadcasted_iota(jnp.int32, other.shape, 1)
    return gram[:half] + jnp.where(lane < half, other, -other)


def diagonal(out):
    row = lax.broadcasted_iota(jnp.int32, out.shape, 0)
    lane = lax.broadcasted_iota(jnp.int32, out.shape, 1)
    return jnp.sum(jnp.where(row == lane, out, 0.0), axis=0, keepdims=True)


def two_traces(first, second):
    return diagonal(first) + pltpu.roll(diagonal(second), BLOCKS, 1)


def by_core(rows, core):
    for y in range(4):
        even, odd = rows[16 * y : 16 * y + 8], rows[16 * y + 8 : 16 * y + 16]
        yield y, jnp.where(core == 0, even, odd), jnp.where(core == 0, odd, even)


def points_kernel(where_ref, t_ref, x_ref, c_ref, near_ref, far_ref, s_ref):
    tm_count, pts = x_ref.shape[0], x_ref.shape[1]
    tiles = s_ref.shape[0]
    table = split(t_ref[...])
    blank = jnp.zeros((tiles * LANES - pts, NFFT), F32)

    def transform(j, samples):
        got = dot3(table, split(jnp.concatenate([samples, blank], axis=0)), NT)
        for n in range(tiles):
            s_ref.at[n][pl.ds(j, 2 * NBINS, stride=BLOCKS), :] = lane_tile(got, n)

    def both(t, following):
        x = x_ref[t]
        transform(2 * t, x)
        transform(2 * t + 1, jnp.concatenate([x[:, HOP:], following], axis=1))

    def four(i, carry):
        for n in range(4):
            both(4 * i + n, x_ref[4 * i + n + 1][:, :HOP])
        return carry

    lax.fori_loop(0, tm_count // 4 - 1, four, 0)
    for t in range(tm_count - 4, tm_count - 1):
        both(t, x_ref[t + 1][:, :HOP])
    both(tm_count - 1, c_ref[...])

    y_at, core, x_at = (where_ref[n] for n in range(3))

    def owner(t):
        xr = lax.rem(t // 8 - x_at + 4, 4)
        z = lax.rem(t, 8)
        outs = []
        for b in range(2):
            mine = pl.ds(pl.multiple_of(2 * BLOCKS * (2 * t + b), 2 * BLOCKS), 2 * BLOCKS)
            rows = split(jnp.concatenate([s_ref[n, mine] for n in range(tiles)], axis=1))
            outs.append(re_im(dot3(rows, rows, NT)))
        for b in range(2):
            for y, near, far in by_core(outs[b], core):
                yr = lax.rem(y - y_at + 4, 4)
                near_ref[yr, xr, 2 * z + b] = near
                far_ref[yr, xr, 2 * z + b] = far
        traces = two_traces(*outs)
        for y in range(4):
            near_ref[y, xr, 16, pl.ds(z, 1), :] = traces
            far_ref[y, xr, 16, pl.ds(z, 1), :] = traces

    def four_owners(i, carry):
        for n in range(4):
            owner(4 * i + n)
        return carry

    lax.fori_loop(0, tm_count // 4, four_owners, 0)


def points_gram(where, table, samples, closing):
    wide = -(-samples.shape[1] // NFFT) * NFFT
    vmem = pl.BlockSpec(memory_space=pltpu.VMEM)
    return pl.pallas_call(
        points_kernel,
        in_specs=[pl.BlockSpec(memory_space=pltpu.SMEM), vmem, vmem, vmem],
        out_specs=(vmem, vmem),
        out_shape=(jax.ShapeDtypeStruct((4, 4, 17, 8, LANES), F32),) * 2,
        scratch_shapes=[pltpu.VMEM((wide // LANES, 2 * NBINS * BLOCKS, LANES), F32)],
        cost_estimate=pl.CostEstimate(
            flops=6 * 10**9, bytes_accessed=20 * 10**6, transcendentals=0
        ),
        compiler_params=pltpu.CompilerParams(vmem_limit_bytes=VMEM_BYTES),
        name="points_gram",
    )(where, table, samples, closing)


def bins_kernel(where_ref, a_ref, near_ref, far_ref, s_ref):
    tiles = s_ref.shape[0]
    tm_count = a_ref.shape[0] // (8 * tiles)
    for n in range(tiles):
        for c in range(4):
            for e in range(2):
                got = a_ref[pl.ds(8 * n + 2 * c + e, tm_count, stride=8 * tiles), :]
                if e == 1 and n >= tiles // 2:
                    got = pltpu.roll(got, tm_count - 1, 0)
                s_ref.at[n][pl.ds(c * BLOCKS + e, tm_count, stride=2), :] = got
    outs = []
    for b in range(2):
        mine = pl.ds(2 * BLOCKS * b, 2 * BLOCKS)
        rows = split(jnp.concatenate([s_ref[n, mine] for n in range(tiles)], axis=1))
        outs.append(re_im(dot3(rows, rows, NT)))
    y_at, core = where_ref[0], where_ref[1]
    for b in range(2):
        for y, near, far in by_core(outs[b], core):
            yr = lax.rem(y - y_at + 4, 4)
            near_ref[yr, b] = near
            far_ref[yr, b] = far
    traces = jnp.broadcast_to(two_traces(*outs), (8, LANES))
    for y in range(4):
        near_ref[y, 2] = traces
        far_ref[y, 2] = traces


def bins_gram(where, coef):
    vmem = pl.BlockSpec(memory_space=pltpu.VMEM)
    tiles = coef.shape[1]
    return pl.pallas_call(
        bins_kernel,
        in_specs=[pl.BlockSpec(memory_space=pltpu.SMEM), vmem],
        out_specs=(vmem, vmem),
        out_shape=(jax.ShapeDtypeStruct((4, 3, 8, LANES), F32),) * 2,
        scratch_shapes=[pltpu.VMEM((tiles, 4 * BLOCKS, LANES), F32)],
        cost_estimate=pl.CostEstimate(
            flops=5 * 10**8, bytes_accessed=2 * 10**6, transcendentals=0
        ),
        compiler_params=pltpu.CompilerParams(vmem_limit_bytes=VMEM_BYTES),
        name="bins_gram",
    )(where, coef.reshape(-1, LANES))


def norm_kernel(where_ref, r_ref, *refs):
    o_ref = refs[-1]
    total = r_ref[0]
    for z in range(1, 8):
        total = total + r_ref[z]
    for ref in refs[:-1]:
        total = total + ref[...]
    row = lax.broadcasted_iota(jnp.int32, (8, LANES), 0)
    lane = lax.broadcasted_iota(jnp.int32, (8, LANES), 1)
    for b in range(2):
        mine = (row == where_ref[3]) & (lane // BLOCKS == b)
        energy = jnp.sum(jnp.where(mine, total[2], 0.0), keepdims=True)
        out = total[b] * (BLOCKS / energy)
        o_ref[b, 0] = out[:, :BLOCKS]
        o_ref[b, 1] = out[:, BLOCKS:]


def normalized(where, parts, others):
    vmem = pl.BlockSpec(memory_space=pltpu.VMEM)
    return pl.pallas_call(
        norm_kernel,
        in_specs=[pl.BlockSpec(memory_space=pltpu.SMEM)] + [vmem] * (1 + len(others)),
        out_specs=vmem,
        out_shape=jax.ShapeDtypeStruct((2, 2, 8, BLOCKS), F32),
        compiler_params=pltpu.CompilerParams(vmem_limit_bytes=VMEM_BYTES),
        name="normalize",
    )(where, parts, *others)


def by_y(d):
    return [(2 * y + c, 2 * ((y + d) % 4) + c) for y in range(4) for c in range(2)]


def by_x(d):
    return [(8 * x + z, 8 * ((x + d) % 4) + z) for x in range(4) for z in range(8)]


def sent_on(near, axis, pairs):
    return [near(0)] + [lax.ppermute(near(d), axis, pairs(d)) for d in range(1, 4)]


def over_space(near, far):
    far = lax.ppermute(far, "space", [(s, s ^ 1) for s in range(8)])
    return sent_on(lambda d: near[d] + far[d], "space", by_y)


def odd_blocks(snapshots, closing, tm, tm_count, first):
    middle = (first + snapshots.shape[1]) // 2
    down = lax.ppermute(
        snapshots[:HOP, first:middle], "tm", [(t, t - 1) for t in range(1, tm_count)]
    )
    up = lax.ppermute(
        snapshots[HOP:, middle:], "tm", [(t, (t + 1) % tm_count) for t in range(tm_count)]
    )

    def finish(down, up):
        after = jnp.where(tm == tm_count - 1, closing[:, first:middle], down)
        ending = jnp.where(tm == 0, closing[:, middle:], snapshots[:HOP, middle:])
        return jnp.concatenate(
            [
                jnp.concatenate([snapshots[HOP:, first:middle], after], axis=0),
                jnp.concatenate([up, ending], axis=0),
            ],
            axis=1,
        )

    return down, up, finish


def body(snapshots, closing, weights, bin_index):
    tm_count = lax.axis_size("tm")
    tm, space = lax.axis_index("tm"), lax.axis_index("space")
    where = jnp.stack([space // 2, space % 2, tm // 8, tm % 8]).astype(jnp.int32)
    first = tm_count * PTS_TM
    roots = jnp.sqrt(weights)[None, :]
    down, up, finish = odd_blocks(snapshots, closing, tm, tm_count, first)
    sent = turned(snapshots, roots, first).reshape(tm_count, PTS_TM, NFFT)
    sent, down, up = lax.optimization_barrier((sent, down, up))
    samples = lax.all_to_all(sent, "tm", 0, 0, tiled=True)
    table = table_rows(bin_index, NFFT)
    coef = coefs(table, roots, snapshots, finish(down, up), first)
    own_roots = lax.dynamic_slice(roots, (0, tm * PTS_TM), (1, PTS_TM))
    own_closing = lax.dynamic_slice(closing, (0, tm * PTS_TM), (HOP, PTS_TM)) * own_roots
    samples, coef, own_closing = lax.optimization_barrier((samples, coef, own_closing.T))
    by_bin = lax.all_to_all(coef, "tm", 0, 0, tiled=True)
    held = sum(over_space(*points_gram(where, table, samples, own_closing)))
    held = sum(sent_on(lambda d: held[d], "tm", by_x))
    by_bin, held = lax.optimization_barrier((by_bin, held))
    traces = jnp.broadcast_to(held[16:], (8, 1, 8, LANES))
    held = jnp.concatenate([held[:16].reshape(8, 2, 8, LANES), traces], axis=1)
    columns = [[8 * x + z for z in range(8)] for x in range(4)]
    others = lax.all_to_all(held, "tm", 0, 0, tiled=True, axis_index_groups=columns)
    return normalized(where, others, over_space(*bins_gram(where, by_bin)))


def solution(mesh):
    return jax.shard_map(
        body,
        mesh=mesh,
        in_specs=(P("tm", "space"), P(None, "space"), P("space"), P()),
        out_specs=P("tm", None, "space", None),
        check_vma=False,
    )
```

```python
import math

import jax
import jax.numpy as jnp
from jax import lax
from jax.experimental import pallas as pl
from jax.experimental.pallas import tpu as pltpu
from jax.sharding import PartitionSpec as P

NFFT = 256
NBINS = 64
HOP = NFFT // 2
BLOCKS = 64
LANES = 128
PTS_TM = 168
F32, BF16 = jnp.float32, jnp.bfloat16
VMEM_BYTES = 50 * 2**20
LONG = 4 * 10**11


def split(a):
    hi = a.astype(BF16)
    return hi, (a - hi.astype(F32)).astype(BF16)


def dot3(a, b, dims):
    dg = lambda u, v: lax.dot_general(u, v, (dims, ((), ())), preferred_element_type=F32)
    return dg(a[0], b[0]) + dg(a[0], b[1]) + dg(a[1], b[0])


NN, NT = ((1,), (0,)), ((1,), (1,))


def table_rows(bin_index, length):
    sample = jnp.arange(length, dtype=jnp.int32)
    window = 0.5 - 0.5 * jnp.cos(2.0 * jnp.pi * sample.astype(F32) / length)
    turns = sample[None, :] * bin_index[:, None] % length
    angle = 2.0 * jnp.pi * turns.astype(F32) / length
    paired = jnp.stack([window * jnp.cos(angle), -window * jnp.sin(angle)], axis=1)
    return paired.reshape(2 * bin_index.shape[0], length)


def widest(cols):
    return max(n * LANES for n in range(1, 7) if cols % (n * LANES) == 0)


def turn_kernel(x_ref, w_ref, o_ref):
    o_ref[...] = (x_ref[...] * w_ref[...]).T


def turned(x, roots, cols):
    rows, step = x.shape[0], widest(cols)
    return pl.pallas_call(
        turn_kernel,
        grid=(cols // step,),
        in_specs=[
            pl.BlockSpec((rows, step), lambda i: (0, i)),
            pl.BlockSpec((1, step), lambda i: (0, i)),
        ],
        out_specs=pl.BlockSpec((step, rows), lambda i: (i, 0)),
        out_shape=jax.ShapeDtypeStruct((cols, rows), F32),
        cost_estimate=pl.CostEstimate(flops=0, bytes_accessed=8 * rows * cols, transcendentals=0),
        compiler_params=pltpu.CompilerParams(vmem_limit_bytes=VMEM_BYTES),
        name="turn_samples",
    )(x, roots)


def lane_tile(a, n):
    return a[:, n * LANES : (n + 1) * LANES]


def coef_kernel(t_ref, w_ref, x_ref, odd_ref, o_ref, s_ref):
    table = split(t_ref[...])
    tiles = s_ref.shape[0]
    for e, part in enumerate((x_ref, odd_ref)):
        got = dot3(table, split(part[...] * w_ref[...]), NN)
        for n in range(tiles):
            s_ref.at[n][pl.ds(e, 2 * NBINS, stride=2), :] = lane_tile(got, n)
    for n in range(tiles):
        o_ref[:, n] = s_ref[n].reshape(-1, 8, LANES)


def coefs(table, roots, x, odd, first):
    rows, cols = x.shape[0], x.shape[1] - first
    step = widest(math.gcd(first, cols))
    return pl.pallas_call(
        coef_kernel,
        grid=(cols // step,),
        in_specs=[
            pl.BlockSpec((2 * NBINS, rows), lambda i: (0, 0)),
            pl.BlockSpec((1, step), lambda i: (0, first // step + i)),
            pl.BlockSpec((rows, step), lambda i: (0, first // step + i)),
            pl.BlockSpec((rows, step), lambda i: (0, i)),
        ],
        out_specs=pl.BlockSpec((NBINS // 2, step // LANES, 8, LANES), lambda i: (0, i, 0, 0)),
        out_shape=jax.ShapeDtypeStruct((NBINS // 2, cols // LANES, 8, LANES), F32),
        scratch_shapes=[pltpu.VMEM((step // LANES, 4 * NBINS, LANES), F32)],
        cost_estimate=pl.CostEstimate(
            flops=LONG, bytes_accessed=10 * rows * cols, transcendentals=0
        ),
        compiler_params=pltpu.CompilerParams(vmem_limit_bytes=VMEM_BYTES),
        name="coefs_by_bin",
    )(table, roots, x, odd)


def re_im(gram):
    half = gram.shape[0] // 2
    other = pltpu.roll(gram[half:], half, 1)
    lane = lax.broadcasted_iota(jnp.int32, other.shape, 1)
    return gram[:half] + jnp.where(lane < half, other, -other)


def diagonal(out):
    row = lax.broadcasted_iota(jnp.int32, out.shape, 0)
    lane = lax.broadcasted_iota(jnp.int32, out.shape, 1)
    return jnp.sum(jnp.where(row == lane, out, 0.0), axis=0, keepdims=True)


def two_traces(first, second):
    return diagonal(first) + pltpu.roll(diagonal(second), BLOCKS, 1)


def by_core(rows, core):
    for y in range(4):
        even, odd = rows[16 * y : 16 * y + 8], rows[16 * y + 8 : 16 * y + 16]
        yield y, jnp.where(core == 0, even, odd), jnp.where(core == 0, odd, even)


def points_kernel(where_ref, t_ref, x_ref, c_ref, near_ref, far_ref, s_ref):
    tm_count, pts = x_ref.shape[0], x_ref.shape[1]
    tiles = s_ref.shape[0]
    table = split(t_ref[...])
    blank = jnp.zeros((tiles * LANES - pts, NFFT), F32)

    def transform(j, samples):
        got = dot3(table, split(jnp.concatenate([samples, blank], axis=0)), NT)
        for n in range(tiles):
            s_ref.at[n][pl.ds(j, 2 * NBINS, stride=BLOCKS), :] = lane_tile(got, n)

    def both(t, following):
        x = x_ref[t]
        transform(2 * t, x)
        transform(2 * t + 1, jnp.concatenate([x[:, HOP:], following], axis=1))

    def four(i, carry):
        for n in range(4):
            both(4 * i + n, x_ref[4 * i + n + 1][:, :HOP])
        return carry

    lax.fori_loop(0, tm_count // 4 - 1, four, 0)
    for t in range(tm_count - 4, tm_count - 1):
        both(t, x_ref[t + 1][:, :HOP])
    both(tm_count - 1, c_ref[...])

    y_at, core, x_at = (where_ref[n] for n in range(3))

    def owner(t):
        xr = lax.rem(t // 8 - x_at + 4, 4)
        z = lax.rem(t, 8)
        outs = []
        for b in range(2):
            mine = pl.ds(pl.multiple_of(2 * BLOCKS * (2 * t + b), 2 * BLOCKS), 2 * BLOCKS)
            rows = split(jnp.concatenate([s_ref[n, mine] for n in range(tiles)], axis=1))
            outs.append(re_im(dot3(rows, rows, NT)))
        for b in range(2):
            for y, near, far in by_core(outs[b], core):
                yr = lax.rem(y - y_at + 4, 4)
                near_ref[yr, xr, 2 * z + b] = near
                far_ref[yr, xr, 2 * z + b] = far
        traces = two_traces(*outs)
        for y in range(4):
            near_ref[y, xr, 16, pl.ds(z, 1), :] = traces
            far_ref[y, xr, 16, pl.ds(z, 1), :] = traces

    def four_owners(i, carry):
        for n in range(4):
            owner(4 * i + n)
        return carry

    lax.fori_loop(0, tm_count // 4, four_owners, 0)


def points_gram(where, table, samples, closing):
    wide = -(-samples.shape[1] // NFFT) * NFFT
    vmem = pl.BlockSpec(memory_space=pltpu.VMEM)
    return pl.pallas_call(
        points_kernel,
        in_specs=[pl.BlockSpec(memory_space=pltpu.SMEM), vmem, vmem, vmem],
        out_specs=(vmem, vmem),
        out_shape=(jax.ShapeDtypeStruct((4, 4, 17, 8, LANES), F32),) * 2,
        scratch_shapes=[pltpu.VMEM((wide // LANES, 2 * NBINS * BLOCKS, LANES), F32)],
        cost_estimate=pl.CostEstimate(
            flops=6 * 10**9, bytes_accessed=20 * 10**6, transcendentals=0
        ),
        compiler_params=pltpu.CompilerParams(vmem_limit_bytes=VMEM_BYTES),
        name="points_gram",
    )(where, table, samples, closing)


def bins_kernel(where_ref, a_ref, near_ref, far_ref, s_ref):
    tiles = s_ref.shape[0]
    tm_count = a_ref.shape[0] // (8 * tiles)
    for n in range(tiles):
        for c in range(4):
            for e in range(2):
                got = a_ref[pl.ds(8 * n + 2 * c + e, tm_count, stride=8 * tiles), :]
                if e == 1 and n >= tiles // 2:
                    got = pltpu.roll(got, tm_count - 1, 0)
                s_ref.at[n][pl.ds(c * BLOCKS + e, tm_count, stride=2), :] = got
    outs = []
    for b in range(2):
        mine = pl.ds(2 * BLOCKS * b, 2 * BLOCKS)
        rows = split(jnp.concatenate([s_ref[n, mine] for n in range(tiles)], axis=1))
        outs.append(re_im(dot3(rows, rows, NT)))
    y_at, core = where_ref[0], where_ref[1]
    for b in range(2):
        for y, near, far in by_core(outs[b], core):
            yr = lax.rem(y - y_at + 4, 4)
            near_ref[yr, b] = near
            far_ref[yr, b] = far
    traces = jnp.broadcast_to(two_traces(*outs), (8, LANES))
    for y in range(4):
        near_ref[y, 2] = traces
        far_ref[y, 2] = traces


def bins_gram(where, coef):
    vmem = pl.BlockSpec(memory_space=pltpu.VMEM)
    tiles = coef.shape[1]
    return pl.pallas_call(
        bins_kernel,
        in_specs=[pl.BlockSpec(memory_space=pltpu.SMEM), vmem],
        out_specs=(vmem, vmem),
        out_shape=(jax.ShapeDtypeStruct((4, 3, 8, LANES), F32),) * 2,
        scratch_shapes=[pltpu.VMEM((tiles, 4 * BLOCKS, LANES), F32)],
        cost_estimate=pl.CostEstimate(
            flops=5 * 10**8, bytes_accessed=2 * 10**6, transcendentals=0
        ),
        compiler_params=pltpu.CompilerParams(vmem_limit_bytes=VMEM_BYTES),
        name="bins_gram",
    )(where, coef.reshape(-1, LANES))


def norm_kernel(where_ref, r_ref, *refs):
    o_ref = refs[-1]
    total = r_ref[0]
    for z in range(1, 8):
        total = total + r_ref[z]
    for ref in refs[:-1]:
        total = total + ref[...]
    row = lax.broadcasted_iota(jnp.int32, (8, LANES), 0)
    lane = lax.broadcasted_iota(jnp.int32, (8, LANES), 1)
    for b in range(2):
        mine = (row == where_ref[3]) & (lane // BLOCKS == b)
        energy = jnp.sum(jnp.where(mine, total[2], 0.0), keepdims=True)
        out = total[b] * (BLOCKS / energy)
        o_ref[b, 0] = out[:, :BLOCKS]
        o_ref[b, 1] = out[:, BLOCKS:]


def normalized(where, parts, others):
    vmem = pl.BlockSpec(memory_space=pltpu.VMEM)
    return pl.pallas_call(
        norm_kernel,
        in_specs=[pl.BlockSpec(memory_space=pltpu.SMEM)] + [vmem] * (1 + len(others)),
        out_specs=vmem,
        out_shape=jax.ShapeDtypeStruct((2, 2, 8, BLOCKS), F32),
        compiler_params=pltpu.CompilerParams(vmem_limit_bytes=VMEM_BYTES),
        name="normalize",
    )(where, parts, *others)


def by_y(d):
    return [(2 * y + c, 2 * ((y + d) % 4) + c) for y in range(4) for c in range(2)]


def by_x(d):
    return [(8 * x + z, 8 * ((x + d) % 4) + z) for x in range(4) for z in range(8)]


def sent_on(near, axis, pairs):
    return [near(0)] + [lax.ppermute(near(d), axis, pairs(d)) for d in range(1, 4)]


def over_space(near, far):
    far = lax.ppermute(far, "space", [(s, s ^ 1) for s in range(8)])
    return sent_on(lambda d: near[d] + far[d], "space", by_y)


def odd_blocks(snapshots, closing, tm, tm_count, first):
    middle = (first + snapshots.shape[1]) // 2
    down = lax.ppermute(
        snapshots[:HOP, first:middle], "tm", [(t, t - 1) for t in range(1, tm_count)]
    )
    up = lax.ppermute(
        snapshots[HOP:, middle:], "tm", [(t, (t + 1) % tm_count) for t in range(tm_count)]
    )

    def finish(down, up):
        after = jnp.where(tm == tm_count - 1, closing[:, first:middle], down)
        ending = jnp.where(tm == 0, closing[:, middle:], snapshots[:HOP, middle:])
        return jnp.concatenate(
            [
                jnp.concatenate([snapshots[HOP:, first:middle], after], axis=0),
                jnp.concatenate([up, ending], axis=0),
            ],
            axis=1,
        )

    return down, up, finish


def body(snapshots, closing, weights, bin_index):
    tm_count = lax.axis_size("tm")
    tm, space = lax.axis_index("tm"), lax.axis_index("space")
    where = jnp.stack([space // 2, space % 2, tm // 8, tm % 8]).astype(jnp.int32)
    first = tm_count * PTS_TM
    roots = jnp.sqrt(weights)[None, :]
    down, up, finish = odd_blocks(snapshots, closing, tm, tm_count, first)
    table = table_rows(bin_index, NFFT)
    own_roots = lax.dynamic_slice(roots, (0, tm * PTS_TM), (1, PTS_TM))
    own_closing = (lax.dynamic_slice(closing, (0, tm * PTS_TM), (HOP, PTS_TM)) * own_roots).T
    roots, table, own_closing, where = lax.optimization_barrier(
        (roots, table, own_closing, where)
    )
    sent = turned(snapshots, roots, first).reshape(tm_count, PTS_TM, NFFT)
    samples = lax.all_to_all(sent, "tm", 0, 0, tiled=True)
    coef = coefs(table, roots, snapshots, finish(down, up), first)
    samples, coef = lax.optimization_barrier((samples, coef))
    by_bin = lax.all_to_all(coef, "tm", 0, 0, tiled=True)
    held = sum(over_space(*points_gram(where, table, samples, own_closing)))
    held = sum(sent_on(lambda d: held[d], "tm", by_x))
    by_bin, held = lax.optimization_barrier((by_bin, held))
    traces = jnp.broadcast_to(held[16:], (8, 1, 8, LANES))
    held = jnp.concatenate([held[:16].reshape(8, 2, 8, LANES), traces], axis=1)
    columns = [[8 * x + z for z in range(8)] for x in range(4)]
    others = lax.all_to_all(held, "tm", 0, 0, tiled=True, axis_index_groups=columns)
    return normalized(where, others, over_space(*bins_gram(where, by_bin)))


def solution(mesh):
    return jax.shard_map(
        body,
        mesh=mesh,
        in_specs=(P("tm", "space"), P(None, "space"), P("space"), P()),
        out_specs=P("tm", None, "space", None),
        check_vma=False,
    )
```

```python
import math

import jax
import jax.numpy as jnp
from jax import lax
from jax.experimental import pallas as pl
from jax.experimental.pallas import tpu as pltpu
from jax.sharding import PartitionSpec as P

NFFT = 256
NBINS = 64
HOP = NFFT // 2
BLOCKS = 64
LANES = 128
PTS_TM = 168
F32, BF16 = jnp.float32, jnp.bfloat16
VMEM_BYTES = 50 * 2**20
LONG = 4 * 10**11


def split(a):
    hi = a.astype(BF16)
    return hi, (a - hi.astype(F32)).astype(BF16)


def dot3(a, b, dims):
    dg = lambda u, v: lax.dot_general(u, v, (dims, ((), ())), preferred_element_type=F32)
    return dg(a[0], b[0]) + dg(a[0], b[1]) + dg(a[1], b[0])


NN, NT = ((1,), (0,)), ((1,), (1,))


def table_rows(bin_index, length):
    sample = jnp.arange(length, dtype=jnp.int32)
    window = 0.5 - 0.5 * jnp.cos(2.0 * jnp.pi * sample.astype(F32) / length)
    turns = sample[None, :] * bin_index[:, None] % length
    angle = 2.0 * jnp.pi * turns.astype(F32) / length
    paired = jnp.stack([window * jnp.cos(angle), -window * jnp.sin(angle)], axis=1)
    return paired.reshape(2 * bin_index.shape[0], length)


def widest(cols, most):
    return max(n * LANES for n in range(1, most + 1) if cols % (n * LANES) == 0)


def turn_kernel(x_ref, w_ref, o_ref):
    o_ref[...] = (x_ref[...] * w_ref[...]).T


def turned(x, roots, cols):
    rows, step = x.shape[0], widest(cols, 24)
    return pl.pallas_call(
        turn_kernel,
        grid=(cols // step,),
        in_specs=[
            pl.BlockSpec((rows, step), lambda i: (0, i)),
            pl.BlockSpec((1, step), lambda i: (0, i)),
        ],
        out_specs=pl.BlockSpec((step, rows), lambda i: (i, 0)),
        out_shape=jax.ShapeDtypeStruct((cols, rows), F32),
        cost_estimate=pl.CostEstimate(flops=0, bytes_accessed=8 * rows * cols, transcendentals=0),
        compiler_params=pltpu.CompilerParams(vmem_limit_bytes=VMEM_BYTES),
        name="turn_samples",
    )(x, roots)


def lane_tile(a, n):
    return a[:, n * LANES : (n + 1) * LANES]


def coef_kernel(t_ref, w_ref, x_ref, odd_ref, o_ref, s_ref):
    table = split(t_ref[...])
    tiles = s_ref.shape[0]
    for e, part in enumerate((x_ref, odd_ref)):
        got = dot3(table, split(part[...] * w_ref[...]), NN)
        for n in range(tiles):
            s_ref.at[n][pl.ds(e, 2 * NBINS, stride=2), :] = lane_tile(got, n)
    for n in range(tiles):
        o_ref[:, n] = s_ref[n].reshape(-1, 8, LANES)


def coefs(table, roots, x, odd, first):
    rows, cols = x.shape[0], x.shape[1] - first
    step = widest(math.gcd(first, cols), 6)
    return pl.pallas_call(
        coef_kernel,
        grid=(cols // step,),
        in_specs=[
            pl.BlockSpec((2 * NBINS, rows), lambda i: (0, 0)),
            pl.BlockSpec((1, step), lambda i: (0, first // step + i)),
            pl.BlockSpec((rows, step), lambda i: (0, first // step + i)),
            pl.BlockSpec((rows, step), lambda i: (0, i)),
        ],
        out_specs=pl.BlockSpec((NBINS // 2, step // LANES, 8, LANES), lambda i: (0, i, 0, 0)),
        out_shape=jax.ShapeDtypeStruct((NBINS // 2, cols // LANES, 8, LANES), F32),
        scratch_shapes=[pltpu.VMEM((step // LANES, 4 * NBINS, LANES), F32)],
        cost_estimate=pl.CostEstimate(
            flops=LONG, bytes_accessed=10 * rows * cols, transcendentals=0
        ),
        compiler_params=pltpu.CompilerParams(vmem_limit_bytes=VMEM_BYTES),
        name="coefs_by_bin",
    )(table, roots, x, odd)


def re_im(gram):
    half = gram.shape[0] // 2
    other = pltpu.roll(gram[half:], half, 1)
    lane = lax.broadcasted_iota(jnp.int32, other.shape, 1)
    return gram[:half] + jnp.where(lane < half, other, -other)


def diagonal(out):
    row = lax.broadcasted_iota(jnp.int32, out.shape, 0)
    lane = lax.broadcasted_iota(jnp.int32, out.shape, 1)
    return jnp.sum(jnp.where(row == lane, out, 0.0), axis=0, keepdims=True)


def two_traces(first, second):
    return diagonal(first) + pltpu.roll(diagonal(second), BLOCKS, 1)


def by_core(rows, core):
    for y in range(4):
        even, odd = rows[16 * y : 16 * y + 8], rows[16 * y + 8 : 16 * y + 16]
        yield y, jnp.where(core == 0, even, odd), jnp.where(core == 0, odd, even)


def points_kernel(where_ref, t_ref, x_ref, c_ref, near_ref, far_ref, s_ref):
    tm_count, pts = x_ref.shape[0], x_ref.shape[1]
    tiles = s_ref.shape[0]
    table = split(t_ref[...])
    blank = jnp.zeros((tiles * LANES - pts, NFFT), F32)

    def transform(j, samples):
        got = dot3(table, split(jnp.concatenate([samples, blank], axis=0)), NT)
        for n in range(tiles):
            s_ref.at[n][pl.ds(j, 2 * NBINS, stride=BLOCKS), :] = lane_tile(got, n)

    def both(t, following):
        x = x_ref[t]
        transform(2 * t, x)
        transform(2 * t + 1, jnp.concatenate([x[:, HOP:], following], axis=1))

    def four(i, carry):
        for n in range(4):
            both(4 * i + n, x_ref[4 * i + n + 1][:, :HOP])
        return carry

    lax.fori_loop(0, tm_count // 4 - 1, four, 0)
    for t in range(tm_count - 4, tm_count - 1):
        both(t, x_ref[t + 1][:, :HOP])
    both(tm_count - 1, c_ref[...])

    y_at, core, x_at = (where_ref[n] for n in range(3))

    def owner(t):
        xr = lax.rem(t // 8 - x_at + 4, 4)
        z = lax.rem(t, 8)
        outs = []
        for b in range(2):
            mine = pl.ds(pl.multiple_of(2 * BLOCKS * (2 * t + b), 2 * BLOCKS), 2 * BLOCKS)
            rows = split(jnp.concatenate([s_ref[n, mine] for n in range(tiles)], axis=1))
            outs.append(re_im(dot3(rows, rows, NT)))
        for b in range(2):
            for y, near, far in by_core(outs[b], core):
                yr = lax.rem(y - y_at + 4, 4)
                near_ref[yr, xr, 2 * z + b] = near
                far_ref[yr, xr, 2 * z + b] = far
        traces = two_traces(*outs)
        for y in range(4):
            near_ref[y, xr, 16, pl.ds(z, 1), :] = traces
            far_ref[y, xr, 16, pl.ds(z, 1), :] = traces

    def four_owners(i, carry):
        for n in range(4):
            owner(4 * i + n)
        return carry

    lax.fori_loop(0, tm_count // 4, four_owners, 0)


def points_gram(where, table, samples, closing):
    wide = -(-samples.shape[1] // NFFT) * NFFT
    vmem = pl.BlockSpec(memory_space=pltpu.VMEM)
    return pl.pallas_call(
        points_kernel,
        in_specs=[pl.BlockSpec(memory_space=pltpu.SMEM), vmem, vmem, vmem],
        out_specs=(vmem, vmem),
        out_shape=(jax.ShapeDtypeStruct((4, 4, 17, 8, LANES), F32),) * 2,
        scratch_shapes=[pltpu.VMEM((wide // LANES, 2 * NBINS * BLOCKS, LANES), F32)],
        cost_estimate=pl.CostEstimate(
            flops=6 * 10**9, bytes_accessed=20 * 10**6, transcendentals=0
        ),
        compiler_params=pltpu.CompilerParams(vmem_limit_bytes=VMEM_BYTES),
        name="points_gram",
    )(where, table, samples, closing)


def bins_kernel(where_ref, a_ref, near_ref, far_ref, s_ref):
    tiles = s_ref.shape[0]
    tm_count = a_ref.shape[0] // (8 * tiles)
    for n in range(tiles):
        for c in range(4):
            for e in range(2):
                got = a_ref[pl.ds(8 * n + 2 * c + e, tm_count, stride=8 * tiles), :]
                if e == 1 and n >= tiles // 2:
                    got = pltpu.roll(got, tm_count - 1, 0)
                s_ref.at[n][pl.ds(c * BLOCKS + e, tm_count, stride=2), :] = got
    outs = []
    for b in range(2):
        mine = pl.ds(2 * BLOCKS * b, 2 * BLOCKS)
        rows = split(jnp.concatenate([s_ref[n, mine] for n in range(tiles)], axis=1))
        outs.append(re_im(dot3(rows, rows, NT)))
    y_at, core = where_ref[0], where_ref[1]
    for b in range(2):
        for y, near, far in by_core(outs[b], core):
            yr = lax.rem(y - y_at + 4, 4)
            near_ref[yr, b] = near
            far_ref[yr, b] = far
    traces = jnp.broadcast_to(two_traces(*outs), (8, LANES))
    for y in range(4):
        near_ref[y, 2] = traces
        far_ref[y, 2] = traces


def bins_gram(where, coef):
    vmem = pl.BlockSpec(memory_space=pltpu.VMEM)
    tiles = coef.shape[1]
    return pl.pallas_call(
        bins_kernel,
        in_specs=[pl.BlockSpec(memory_space=pltpu.SMEM), vmem],
        out_specs=(vmem, vmem),
        out_shape=(jax.ShapeDtypeStruct((4, 3, 8, LANES), F32),) * 2,
        scratch_shapes=[pltpu.VMEM((tiles, 4 * BLOCKS, LANES), F32)],
        cost_estimate=pl.CostEstimate(
            flops=5 * 10**8, bytes_accessed=2 * 10**6, transcendentals=0
        ),
        compiler_params=pltpu.CompilerParams(vmem_limit_bytes=VMEM_BYTES),
        name="bins_gram",
    )(where, coef.reshape(-1, LANES))


def norm_kernel(where_ref, r_ref, *refs):
    o_ref = refs[-1]
    total = r_ref[0]
    for z in range(1, 8):
        total = total + r_ref[z]
    for ref in refs[:-1]:
        total = total + ref[...]
    row = lax.broadcasted_iota(jnp.int32, (8, LANES), 0)
    lane = lax.broadcasted_iota(jnp.int32, (8, LANES), 1)
    for b in range(2):
        mine = (row == where_ref[3]) & (lane // BLOCKS == b)
        energy = jnp.sum(jnp.where(mine, total[2], 0.0), keepdims=True)
        out = total[b] * (BLOCKS / energy)
        o_ref[b, 0] = out[:, :BLOCKS]
        o_ref[b, 1] = out[:, BLOCKS:]


def normalized(where, parts, others):
    vmem = pl.BlockSpec(memory_space=pltpu.VMEM)
    return pl.pallas_call(
        norm_kernel,
        in_specs=[pl.BlockSpec(memory_space=pltpu.SMEM)] + [vmem] * (1 + len(others)),
        out_specs=vmem,
        out_shape=jax.ShapeDtypeStruct((2, 2, 8, BLOCKS), F32),
        compiler_params=pltpu.CompilerParams(vmem_limit_bytes=VMEM_BYTES),
        name="normalize",
    )(where, parts, *others)


def by_y(d):
    return [(2 * y + c, 2 * ((y + d) % 4) + c) for y in range(4) for c in range(2)]


def by_x(d):
    return [(8 * x + z, 8 * ((x + d) % 4) + z) for x in range(4) for z in range(8)]


def sent_on(near, axis, pairs):
    return [near(0)] + [lax.ppermute(near(d), axis, pairs(d)) for d in range(1, 4)]


def over_space(near, far):
    far = lax.ppermute(far, "space", [(s, s ^ 1) for s in range(8)])
    return sent_on(lambda d: near[d] + far[d], "space", by_y)


def odd_blocks(snapshots, closing, tm, tm_count, first):
    middle = (first + snapshots.shape[1]) // 2
    down = lax.ppermute(
        snapshots[:HOP, first:middle], "tm", [(t, t - 1) for t in range(1, tm_count)]
    )
    up = lax.ppermute(
        snapshots[HOP:, middle:], "tm", [(t, (t + 1) % tm_count) for t in range(tm_count)]
    )

    def finish(down, up):
        after = jnp.where(tm == tm_count - 1, closing[:, first:middle], down)
        ending = jnp.where(tm == 0, closing[:, middle:], snapshots[:HOP, middle:])
        return jnp.concatenate(
            [
                jnp.concatenate([snapshots[HOP:, first:middle], after], axis=0),
                jnp.concatenate([up, ending], axis=0),
            ],
            axis=1,
        )

    return down, up, finish


def body(snapshots, closing, weights, bin_index):
    tm_count = lax.axis_size("tm")
    tm, space = lax.axis_index("tm"), lax.axis_index("space")
    where = jnp.stack([space // 2, space % 2, tm // 8, tm % 8]).astype(jnp.int32)
    first = tm_count * PTS_TM
    roots = jnp.sqrt(weights)[None, :]
    down, up, finish = odd_blocks(snapshots, closing, tm, tm_count, first)
    sent = turned(snapshots, roots, first).reshape(tm_count, PTS_TM, NFFT)
    samples = lax.all_to_all(sent, "tm", 0, 0, tiled=True)
    down, up, bin_index, closing = lax.optimization_barrier((down, up, bin_index, closing))
    table = table_rows(bin_index, NFFT)
    own_roots = lax.dynamic_slice(roots, (0, tm * PTS_TM), (1, PTS_TM))
    own_closing = lax.dynamic_slice(closing, (0, tm * PTS_TM), (HOP, PTS_TM)) * own_roots
    coef = coefs(table, roots, snapshots, finish(down, up), first)
    samples, coef, own_closing = lax.optimization_barrier((samples, coef, own_closing.T))
    by_bin = lax.all_to_all(coef, "tm", 0, 0, tiled=True)
    held = sum(over_space(*points_gram(where, table, samples, own_closing)))
    held = sum(sent_on(lambda d: held[d], "tm", by_x))
    traces = jnp.broadcast_to(held[16:], (8, 1, 8, LANES))
    held = jnp.concatenate([held[:16].reshape(8, 2, 8, LANES), traces], axis=1)
    by_bin, held = lax.optimization_barrier((by_bin, held))
    columns = [[8 * x + z for z in range(8)] for x in range(4)]
    others = lax.all_to_all(held, "tm", 0, 0, tiled=True, axis_index_groups=columns)
    return normalized(where, others, over_space(*bins_gram(where, by_bin)))


def solution(mesh):
    return jax.shard_map(
        body,
        mesh=mesh,
        in_specs=(P("tm", "space"), P(None, "space"), P("space"), P()),
        out_specs=P("tm", None, "space", None),
        check_vma=False,
    )
```

```python
import functools
import math

import jax
import jax.numpy as jnp
from jax import lax
from jax.experimental import pallas as pl
from jax.experimental.pallas import tpu as pltpu
from jax.sharding import PartitionSpec as P

NFFT = 256
NBINS = 64
HOP = NFFT // 2
BLOCKS = 64
LANES = 128
PTS_TM = 168
F32, BF16 = jnp.float32, jnp.bfloat16
VMEM_BYTES = 50 * 2**20
LONG = 4 * 10**11


def split(a):
    hi = a.astype(BF16)
    return hi, (a - hi.astype(F32)).astype(BF16)


def dot3(a, b, dims):
    dg = lambda u, v: lax.dot_general(u, v, (dims, ((), ())), preferred_element_type=F32)
    return dg(a[0], b[0]) + dg(a[0], b[1]) + dg(a[1], b[0])


NN, NT = ((1,), (0,)), ((1,), (1,))


def table_rows(bin_index, length):
    sample = jnp.arange(length, dtype=jnp.int32)
    window = 0.5 - 0.5 * jnp.cos(2.0 * jnp.pi * sample.astype(F32) / length)
    turns = sample[None, :] * bin_index[:, None] % length
    angle = 2.0 * jnp.pi * turns.astype(F32) / length
    paired = jnp.stack([window * jnp.cos(angle), -window * jnp.sin(angle)], axis=1)
    return paired.reshape(2 * bin_index.shape[0], length)


def widest(cols, most):
    return max(n * LANES for n in range(1, most + 1) if cols % (n * LANES) == 0)


def turn_kernel(x_ref, w_ref, o_ref):
    o_ref[...] = (x_ref[...] * w_ref[...]).T


def turned(x, roots, cols):
    rows, step = x.shape[0], widest(cols, 24)
    return pl.pallas_call(
        turn_kernel,
        grid=(cols // step,),
        in_specs=[
            pl.BlockSpec((rows, step), lambda i: (0, i)),
            pl.BlockSpec((1, step), lambda i: (0, i)),
        ],
        out_specs=pl.BlockSpec((step, rows), lambda i: (i, 0)),
        out_shape=jax.ShapeDtypeStruct((cols, rows), F32),
        cost_estimate=pl.CostEstimate(flops=0, bytes_accessed=8 * rows * cols, transcendentals=0),
        compiler_params=pltpu.CompilerParams(vmem_limit_bytes=VMEM_BYTES),
        name="turn_samples",
    )(x, roots)


def halves_kernel(first, middle, x_ref, low_ref, high_ref, sems):
    low = pltpu.make_async_copy(
        x_ref.at[pl.ds(0, HOP), pl.ds(first, middle - first)], low_ref, sems.at[0]
    )
    high = pltpu.make_async_copy(
        x_ref.at[pl.ds(HOP, HOP), pl.ds(middle, x_ref.shape[1] - middle)], high_ref, sems.at[1]
    )
    low.start()
    high.start()
    low.wait()
    high.wait()


def halves(x, first, middle):
    return pl.pallas_call(
        functools.partial(halves_kernel, first, middle),
        in_specs=[pl.BlockSpec(memory_space=pl.ANY)],
        out_specs=(pl.BlockSpec(memory_space=pltpu.VMEM),) * 2,
        out_shape=(
            jax.ShapeDtypeStruct((HOP, middle - first), F32),
            jax.ShapeDtypeStruct((HOP, x.shape[1] - middle), F32),
        ),
        scratch_shapes=[pltpu.SemaphoreType.DMA((2,))],
        compiler_params=pltpu.CompilerParams(vmem_limit_bytes=VMEM_BYTES),
        name="halo_halves",
    )(x)


def lane_tile(a, n):
    return a[:, n * LANES : (n + 1) * LANES]


def coef_kernel(t_ref, w_ref, x_ref, odd_ref, o_ref, s_ref):
    table = split(t_ref[...])
    tiles = s_ref.shape[0]
    for e, part in enumerate((x_ref, odd_ref)):
        got = dot3(table, split(part[...] * w_ref[...]), NN)
        for n in range(tiles):
            s_ref.at[n][pl.ds(e, 2 * NBINS, stride=2), :] = lane_tile(got, n)
    for n in range(tiles):
        o_ref[:, n] = s_ref[n].reshape(-1, 8, LANES)


def coefs(table, roots, x, odd, first):
    rows, cols = x.shape[0], x.shape[1] - first
    step = widest(math.gcd(first, cols), 6)
    return pl.pallas_call(
        coef_kernel,
        grid=(cols // step,),
        in_specs=[
            pl.BlockSpec((2 * NBINS, rows), lambda i: (0, 0)),
            pl.BlockSpec((1, step), lambda i: (0, first // step + i)),
            pl.BlockSpec((rows, step), lambda i: (0, first // step + i)),
            pl.BlockSpec((rows, step), lambda i: (0, i)),
        ],
        out_specs=pl.BlockSpec((NBINS // 2, step // LANES, 8, LANES), lambda i: (0, i, 0, 0)),
        out_shape=jax.ShapeDtypeStruct((NBINS // 2, cols // LANES, 8, LANES), F32),
        scratch_shapes=[pltpu.VMEM((step // LANES, 4 * NBINS, LANES), F32)],
        cost_estimate=pl.CostEstimate(
            flops=LONG, bytes_accessed=10 * rows * cols, transcendentals=0
        ),
        compiler_params=pltpu.CompilerParams(vmem_limit_bytes=VMEM_BYTES),
        name="coefs_by_bin",
    )(table, roots, x, odd)


def re_im(gram):
    half = gram.shape[0] // 2
    other = pltpu.roll(gram[half:], half, 1)
    lane = lax.broadcasted_iota(jnp.int32, other.shape, 1)
    return gram[:half] + jnp.where(lane < half, other, -other)


def diagonal(out):
    row = lax.broadcasted_iota(jnp.int32, out.shape, 0)
    lane = lax.broadcasted_iota(jnp.int32, out.shape, 1)
    return jnp.sum(jnp.where(row == lane, out, 0.0), axis=0, keepdims=True)


def two_traces(first, second):
    return diagonal(first) + pltpu.roll(diagonal(second), BLOCKS, 1)


def by_core(rows, core):
    for y in range(4):
        even, odd = rows[16 * y : 16 * y + 8], rows[16 * y + 8 : 16 * y + 16]
        yield y, jnp.where(core == 0, even, odd), jnp.where(core == 0, odd, even)


def points_kernel(where_ref, t_ref, x_ref, c_ref, near_ref, far_ref, s_ref):
    tm_count, pts = x_ref.shape[0], x_ref.shape[1]
    tiles = s_ref.shape[0]
    table = split(t_ref[...])
    blank = jnp.zeros((tiles * LANES - pts, NFFT), F32)

    def transform(j, samples):
        got = dot3(table, split(jnp.concatenate([samples, blank], axis=0)), NT)
        for n in range(tiles):
            s_ref.at[n][pl.ds(j, 2 * NBINS, stride=BLOCKS), :] = lane_tile(got, n)

    def both(t, following):
        x = x_ref[t]
        transform(2 * t, x)
        transform(2 * t + 1, jnp.concatenate([x[:, HOP:], following], axis=1))

    def four(i, carry):
        for n in range(4):
            both(4 * i + n, x_ref[4 * i + n + 1][:, :HOP])
        return carry

    lax.fori_loop(0, tm_count // 4 - 1, four, 0)
    for t in range(tm_count - 4, tm_count - 1):
        both(t, x_ref[t + 1][:, :HOP])
    both(tm_count - 1, c_ref[...])

    y_at, core, x_at = (where_ref[n] for n in range(3))

    def owner(t):
        xr = lax.rem(t // 8 - x_at + 4, 4)
        z = lax.rem(t, 8)
        outs = []
        for b in range(2):
            mine = pl.ds(pl.multiple_of(2 * BLOCKS * (2 * t + b), 2 * BLOCKS), 2 * BLOCKS)
            rows = split(jnp.concatenate([s_ref[n, mine] for n in range(tiles)], axis=1))
            outs.append(re_im(dot3(rows, rows, NT)))
        for b in range(2):
            for y, near, far in by_core(outs[b], core):
                yr = lax.rem(y - y_at + 4, 4)
                near_ref[yr, xr, 2 * z + b] = near
                far_ref[yr, xr, 2 * z + b] = far
        traces = two_traces(*outs)
        for y in range(4):
            near_ref[y, xr, 16, pl.ds(z, 1), :] = traces
            far_ref[y, xr, 16, pl.ds(z, 1), :] = traces

    def four_owners(i, carry):
        for n in range(4):
            owner(4 * i + n)
        return carry

    lax.fori_loop(0, tm_count // 4, four_owners, 0)


def points_gram(where, table, samples, closing):
    wide = -(-samples.shape[1] // NFFT) * NFFT
    vmem = pl.BlockSpec(memory_space=pltpu.VMEM)
    return pl.pallas_call(
        points_kernel,
        in_specs=[pl.BlockSpec(memory_space=pltpu.SMEM), vmem, vmem, vmem],
        out_specs=(vmem, vmem),
        out_shape=(jax.ShapeDtypeStruct((4, 4, 17, 8, LANES), F32),) * 2,
        scratch_shapes=[pltpu.VMEM((wide // LANES, 2 * NBINS * BLOCKS, LANES), F32)],
        cost_estimate=pl.CostEstimate(
            flops=6 * 10**9, bytes_accessed=20 * 10**6, transcendentals=0
        ),
        compiler_params=pltpu.CompilerParams(vmem_limit_bytes=VMEM_BYTES),
        name="points_gram",
    )(where, table, samples, closing)


def bins_kernel(where_ref, a_ref, near_ref, far_ref, s_ref):
    tiles = s_ref.shape[0]
    tm_count = a_ref.shape[0] // (8 * tiles)
    for n in range(tiles):
        for c in range(4):
            for e in range(2):
                got = a_ref[pl.ds(8 * n + 2 * c + e, tm_count, stride=8 * tiles), :]
                if e == 1 and n >= tiles // 2:
                    got = pltpu.roll(got, tm_count - 1, 0)
                s_ref.at[n][pl.ds(c * BLOCKS + e, tm_count, stride=2), :] = got
    outs = []
    for b in range(2):
        mine = pl.ds(2 * BLOCKS * b, 2 * BLOCKS)
        rows = split(jnp.concatenate([s_ref[n, mine] for n in range(tiles)], axis=1))
        outs.append(re_im(dot3(rows, rows, NT)))
    y_at, core = where_ref[0], where_ref[1]
    for b in range(2):
        for y, near, far in by_core(outs[b], core):
            yr = lax.rem(y - y_at + 4, 4)
            near_ref[yr, b] = near
            far_ref[yr, b] = far
    traces = jnp.broadcast_to(two_traces(*outs), (8, LANES))
    for y in range(4):
        near_ref[y, 2] = traces
        far_ref[y, 2] = traces


def bins_gram(where, coef):
    vmem = pl.BlockSpec(memory_space=pltpu.VMEM)
    tiles = coef.shape[1]
    return pl.pallas_call(
        bins_kernel,
        in_specs=[pl.BlockSpec(memory_space=pltpu.SMEM), vmem],
        out_specs=(vmem, vmem),
        out_shape=(jax.ShapeDtypeStruct((4, 3, 8, LANES), F32),) * 2,
        scratch_shapes=[pltpu.VMEM((tiles, 4 * BLOCKS, LANES), F32)],
        cost_estimate=pl.CostEstimate(
            flops=5 * 10**8, bytes_accessed=2 * 10**6, transcendentals=0
        ),
        compiler_params=pltpu.CompilerParams(vmem_limit_bytes=VMEM_BYTES),
        name="bins_gram",
    )(where, coef.reshape(-1, LANES))


def norm_kernel(where_ref, r_ref, *refs):
    o_ref = refs[-1]
    total = r_ref[0]
    for z in range(1, 8):
        total = total + r_ref[z]
    for ref in refs[:-1]:
        total = total + ref[...]
    row = lax.broadcasted_iota(jnp.int32, (8, LANES), 0)
    lane = lax.broadcasted_iota(jnp.int32, (8, LANES), 1)
    for b in range(2):
        mine = (row == where_ref[3]) & (lane // BLOCKS == b)
        energy = jnp.sum(jnp.where(mine, total[2], 0.0), keepdims=True)
        out = total[b] * (BLOCKS / energy)
        o_ref[b, 0] = out[:, :BLOCKS]
        o_ref[b, 1] = out[:, BLOCKS:]


def normalized(where, parts, others):
    vmem = pl.BlockSpec(memory_space=pltpu.VMEM)
    return pl.pallas_call(
        norm_kernel,
        in_specs=[pl.BlockSpec(memory_space=pltpu.SMEM)] + [vmem] * (1 + len(others)),
        out_specs=vmem,
        out_shape=jax.ShapeDtypeStruct((2, 2, 8, BLOCKS), F32),
        compiler_params=pltpu.CompilerParams(vmem_limit_bytes=VMEM_BYTES),
        name="normalize",
    )(where, parts, *others)


def by_y(d):
    return [(2 * y + c, 2 * ((y + d) % 4) + c) for y in range(4) for c in range(2)]


def by_x(d):
    return [(8 * x + z, 8 * ((x + d) % 4) + z) for x in range(4) for z in range(8)]


def sent_on(near, axis, pairs):
    return [near(0)] + [lax.ppermute(near(d), axis, pairs(d)) for d in range(1, 4)]


def over_space(near, far):
    far = lax.ppermute(far, "space", [(s, s ^ 1) for s in range(8)])
    return sent_on(lambda d: near[d] + far[d], "space", by_y)


def odd_blocks(snapshots, closing, tm, tm_count, first):
    middle = (first + snapshots.shape[1]) // 2
    low, high = halves(snapshots, first, middle)
    down = lax.ppermute(low, "tm", [(t, t - 1) for t in range(1, tm_count)])
    up = lax.ppermute(high, "tm", [(t, (t + 1) % tm_count) for t in range(tm_count)])

    def finish(down, up):
        after = jnp.where(tm == tm_count - 1, closing[:, first:middle], down)
        ending = jnp.where(tm == 0, closing[:, middle:], snapshots[:HOP, middle:])
        return jnp.concatenate(
            [
                jnp.concatenate([snapshots[HOP:, first:middle], after], axis=0),
                jnp.concatenate([up, ending], axis=0),
            ],
            axis=1,
        )

    return down, up, finish


def body(snapshots, closing, weights, bin_index):
    tm_count = lax.axis_size("tm")
    tm, space = lax.axis_index("tm"), lax.axis_index("space")
    where = jnp.stack([space // 2, space % 2, tm // 8, tm % 8]).astype(jnp.int32)
    first = tm_count * PTS_TM
    roots = jnp.sqrt(weights)[None, :]
    down, up, finish = odd_blocks(snapshots, closing, tm, tm_count, first)
    sent = turned(snapshots, roots, first).reshape(tm_count, PTS_TM, NFFT)
    samples = lax.all_to_all(sent, "tm", 0, 0, tiled=True)
    down, up, bin_index, closing = lax.optimization_barrier((down, up, bin_index, closing))
    table = table_rows(bin_index, NFFT)
    own_roots = lax.dynamic_slice(roots, (0, tm * PTS_TM), (1, PTS_TM))
    own_closing = lax.dynamic_slice(closing, (0, tm * PTS_TM), (HOP, PTS_TM)) * own_roots
    coef = coefs(table, roots, snapshots, finish(down, up), first)
    samples, coef, own_closing = lax.optimization_barrier((samples, coef, own_closing.T))
    by_bin = lax.all_to_all(coef, "tm", 0, 0, tiled=True)
    held = sum(over_space(*points_gram(where, table, samples, own_closing)))
    held = sum(sent_on(lambda d: held[d], "tm", by_x))
    traces = jnp.broadcast_to(held[16:], (8, 1, 8, LANES))
    held = jnp.concatenate([held[:16].reshape(8, 2, 8, LANES), traces], axis=1)
    by_bin, held = lax.optimization_barrier((by_bin, held))
    columns = [[8 * x + z for z in range(8)] for x in range(4)]
    others = lax.all_to_all(held, "tm", 0, 0, tiled=True, axis_index_groups=columns)
    return normalized(where, others, over_space(*bins_gram(where, by_bin)))


def solution(mesh):
    return jax.shard_map(
        body,
        mesh=mesh,
        in_specs=(P("tm", "space"), P(None, "space"), P("space"), P()),
        out_specs=P("tm", None, "space", None),
        check_vma=False,
    )
```

```python
import functools
import math

import jax
import jax.numpy as jnp
from jax import lax
from jax.experimental import pallas as pl
from jax.experimental.pallas import tpu as pltpu
from jax.sharding import PartitionSpec as P

NFFT = 256
NBINS = 64
HOP = NFFT // 2
BLOCKS = 64
LANES = 128
PTS_TM = 168
F32, BF16 = jnp.float32, jnp.bfloat16
VMEM_BYTES = 50 * 2**20
LONG = 4 * 10**11


def split(a):
    hi = a.astype(BF16)
    return hi, (a - hi.astype(F32)).astype(BF16)


def dot3(a, b, dims):
    dg = lambda u, v: lax.dot_general(u, v, (dims, ((), ())), preferred_element_type=F32)
    return dg(a[0], b[0]) + dg(a[0], b[1]) + dg(a[1], b[0])


NN, NT = ((1,), (0,)), ((1,), (1,))


def table_rows(bin_index, length):
    sample = jnp.arange(length, dtype=jnp.int32)
    window = 0.5 - 0.5 * jnp.cos(2.0 * jnp.pi * sample.astype(F32) / length)
    turns = sample[None, :] * bin_index[:, None] % length
    angle = 2.0 * jnp.pi * turns.astype(F32) / length
    paired = jnp.stack([window * jnp.cos(angle), -window * jnp.sin(angle)], axis=1)
    return paired.reshape(2 * bin_index.shape[0], length)


def widest(cols, most):
    return max(n * LANES for n in range(1, most + 1) if cols % (n * LANES) == 0)


def turn_kernel(x_ref, w_ref, o_ref, in_ref, out_ref, in_sems, out_sems):
    step = in_ref.shape[2]
    steps = in_ref.shape[0]
    ins = [
        pltpu.make_async_copy(x_ref.at[:, pl.ds(n * step, step)], in_ref.at[n], in_sems.at[n])
        for n in range(steps)
    ]
    outs = [
        pltpu.make_async_copy(out_ref.at[n], o_ref.at[pl.ds(n * step, step)], out_sems.at[n])
        for n in range(steps)
    ]
    for copy in ins:
        copy.start()
    for n in range(steps):
        ins[n].wait()
        out_ref[n] = (in_ref[n] * w_ref[:, n * step : (n + 1) * step]).T
        outs[n].start()
    for copy in outs:
        copy.wait()


def turned(x, roots, cols):
    rows, step = x.shape[0], widest(cols, 6)
    hbm = pl.BlockSpec(memory_space=pl.ANY)
    return pl.pallas_call(
        turn_kernel,
        in_specs=[hbm, pl.BlockSpec(memory_space=pltpu.VMEM)],
        out_specs=hbm,
        out_shape=jax.ShapeDtypeStruct((cols, rows), F32),
        scratch_shapes=[
            pltpu.VMEM((cols // step, rows, step), F32),
            pltpu.VMEM((cols // step, step, rows), F32),
            pltpu.SemaphoreType.DMA((cols // step,)),
            pltpu.SemaphoreType.DMA((cols // step,)),
        ],
        cost_estimate=pl.CostEstimate(flops=0, bytes_accessed=8 * rows * cols, transcendentals=0),
        compiler_params=pltpu.CompilerParams(vmem_limit_bytes=VMEM_BYTES),
        name="turn_samples",
    )(x, roots)


def halves_kernel(first, middle, x_ref, low_ref, high_ref, sems):
    low = pltpu.make_async_copy(
        x_ref.at[pl.ds(0, HOP), pl.ds(first, middle - first)], low_ref, sems.at[0]
    )
    high = pltpu.make_async_copy(
        x_ref.at[pl.ds(HOP, HOP), pl.ds(middle, x_ref.shape[1] - middle)], high_ref, sems.at[1]
    )
    low.start()
    high.start()
    low.wait()
    high.wait()


def halves(x, first, middle):
    return pl.pallas_call(
        functools.partial(halves_kernel, first, middle),
        in_specs=[pl.BlockSpec(memory_space=pl.ANY)],
        out_specs=(pl.BlockSpec(memory_space=pltpu.VMEM),) * 2,
        out_shape=(
            jax.ShapeDtypeStruct((HOP, middle - first), F32),
            jax.ShapeDtypeStruct((HOP, x.shape[1] - middle), F32),
        ),
        scratch_shapes=[pltpu.SemaphoreType.DMA((2,))],
        compiler_params=pltpu.CompilerParams(vmem_limit_bytes=VMEM_BYTES),
        name="halo_halves",
    )(x)


def lane_tile(a, n):
    return a[:, n * LANES : (n + 1) * LANES]


def coef_kernel(t_ref, w_ref, x_ref, odd_ref, o_ref, s_ref):
    table = split(t_ref[...])
    tiles = s_ref.shape[0]
    for e, part in enumerate((x_ref, odd_ref)):
        got = dot3(table, split(part[...] * w_ref[...]), NN)
        for n in range(tiles):
            s_ref.at[n][pl.ds(e, 2 * NBINS, stride=2), :] = lane_tile(got, n)
    for n in range(tiles):
        o_ref[:, n] = s_ref[n].reshape(-1, 8, LANES)


def coefs(table, roots, x, odd, first):
    rows, cols = x.shape[0], x.shape[1] - first
    step = widest(math.gcd(first, cols), 6)
    return pl.pallas_call(
        coef_kernel,
        grid=(cols // step,),
        in_specs=[
            pl.BlockSpec((2 * NBINS, rows), lambda i: (0, 0)),
            pl.BlockSpec((1, step), lambda i: (0, first // step + i)),
            pl.BlockSpec((rows, step), lambda i: (0, first // step + i)),
            pl.BlockSpec((rows, step), lambda i: (0, i)),
        ],
        out_specs=pl.BlockSpec((NBINS // 2, step // LANES, 8, LANES), lambda i: (0, i, 0, 0)),
        out_shape=jax.ShapeDtypeStruct((NBINS // 2, cols // LANES, 8, LANES), F32),
        scratch_shapes=[pltpu.VMEM((step // LANES, 4 * NBINS, LANES), F32)],
        cost_estimate=pl.CostEstimate(
            flops=LONG, bytes_accessed=10 * rows * cols, transcendentals=0
        ),
        compiler_params=pltpu.CompilerParams(vmem_limit_bytes=VMEM_BYTES),
        name="coefs_by_bin",
    )(table, roots, x, odd)


def re_im(gram):
    half = gram.shape[0] // 2
    other = pltpu.roll(gram[half:], half, 1)
    lane = lax.broadcasted_iota(jnp.int32, other.shape, 1)
    return gram[:half] + jnp.where(lane < half, other, -other)


def diagonal(out):
    row = lax.broadcasted_iota(jnp.int32, out.shape, 0)
    lane = lax.broadcasted_iota(jnp.int32, out.shape, 1)
    return jnp.sum(jnp.where(row == lane, out, 0.0), axis=0, keepdims=True)


def two_traces(first, second):
    return diagonal(first) + pltpu.roll(diagonal(second), BLOCKS, 1)


def by_core(rows, core):
    for y in range(4):
        even, odd = rows[16 * y : 16 * y + 8], rows[16 * y + 8 : 16 * y + 16]
        yield y, jnp.where(core == 0, even, odd), jnp.where(core == 0, odd, even)


def points_kernel(where_ref, t_ref, x_ref, c_ref, near_ref, far_ref, s_ref):
    tm_count, pts = x_ref.shape[0], x_ref.shape[1]
    tiles = s_ref.shape[0]
    table = split(t_ref[...])
    blank = jnp.zeros((tiles * LANES - pts, NFFT), F32)

    def transform(j, samples):
        got = dot3(table, split(jnp.concatenate([samples, blank], axis=0)), NT)
        for n in range(tiles):
            s_ref.at[n][pl.ds(j, 2 * NBINS, stride=BLOCKS), :] = lane_tile(got, n)

    def both(t, following):
        x = x_ref[t]
        transform(2 * t, x)
        transform(2 * t + 1, jnp.concatenate([x[:, HOP:], following], axis=1))

    def four(i, carry):
        for n in range(4):
            both(4 * i + n, x_ref[4 * i + n + 1][:, :HOP])
        return carry

    lax.fori_loop(0, tm_count // 4 - 1, four, 0)
    for t in range(tm_count - 4, tm_count - 1):
        both(t, x_ref[t + 1][:, :HOP])
    both(tm_count - 1, c_ref[...])

    y_at, core, x_at = (where_ref[n] for n in range(3))

    def owner(t):
        xr = lax.rem(t // 8 - x_at + 4, 4)
        z = lax.rem(t, 8)
        outs = []
        for b in range(2):
            mine = pl.ds(pl.multiple_of(2 * BLOCKS * (2 * t + b), 2 * BLOCKS), 2 * BLOCKS)
            rows = split(jnp.concatenate([s_ref[n, mine] for n in range(tiles)], axis=1))
            outs.append(re_im(dot3(rows, rows, NT)))
        for b in range(2):
            for y, near, far in by_core(outs[b], core):
                yr = lax.rem(y - y_at + 4, 4)
                near_ref[yr, xr, 2 * z + b] = near
                far_ref[yr, xr, 2 * z + b] = far
        traces = two_traces(*outs)
        for y in range(4):
            near_ref[y, xr, 16, pl.ds(z, 1), :] = traces
            far_ref[y, xr, 16, pl.ds(z, 1), :] = traces

    def four_owners(i, carry):
        for n in range(4):
            owner(4 * i + n)
        return carry

    lax.fori_loop(0, tm_count // 4, four_owners, 0)


def points_gram(where, table, samples, closing):
    wide = -(-samples.shape[1] // NFFT) * NFFT
    vmem = pl.BlockSpec(memory_space=pltpu.VMEM)
    return pl.pallas_call(
        points_kernel,
        in_specs=[pl.BlockSpec(memory_space=pltpu.SMEM), vmem, vmem, vmem],
        out_specs=(vmem, vmem),
        out_shape=(jax.ShapeDtypeStruct((4, 4, 17, 8, LANES), F32),) * 2,
        scratch_shapes=[pltpu.VMEM((wide // LANES, 2 * NBINS * BLOCKS, LANES), F32)],
        cost_estimate=pl.CostEstimate(
            flops=6 * 10**9, bytes_accessed=20 * 10**6, transcendentals=0
        ),
        compiler_params=pltpu.CompilerParams(vmem_limit_bytes=VMEM_BYTES),
        name="points_gram",
    )(where, table, samples, closing)


def bins_kernel(where_ref, a_ref, near_ref, far_ref, s_ref):
    tiles = s_ref.shape[0]
    tm_count = a_ref.shape[0] // (8 * tiles)
    for n in range(tiles):
        for c in range(4):
            for e in range(2):
                got = a_ref[pl.ds(8 * n + 2 * c + e, tm_count, stride=8 * tiles), :]
                if e == 1 and n >= tiles // 2:
                    got = pltpu.roll(got, tm_count - 1, 0)
                s_ref.at[n][pl.ds(c * BLOCKS + e, tm_count, stride=2), :] = got
    outs = []
    for b in range(2):
        mine = pl.ds(2 * BLOCKS * b, 2 * BLOCKS)
        rows = split(jnp.concatenate([s_ref[n, mine] for n in range(tiles)], axis=1))
        outs.append(re_im(dot3(rows, rows, NT)))
    y_at, core = where_ref[0], where_ref[1]
    for b in range(2):
        for y, near, far in by_core(outs[b], core):
            yr = lax.rem(y - y_at + 4, 4)
            near_ref[yr, b] = near
            far_ref[yr, b] = far
    traces = jnp.broadcast_to(two_traces(*outs), (8, LANES))
    for y in range(4):
        near_ref[y, 2] = traces
        far_ref[y, 2] = traces


def bins_gram(where, coef):
    vmem = pl.BlockSpec(memory_space=pltpu.VMEM)
    tiles = coef.shape[1]
    return pl.pallas_call(
        bins_kernel,
        in_specs=[pl.BlockSpec(memory_space=pltpu.SMEM), vmem],
        out_specs=(vmem, vmem),
        out_shape=(jax.ShapeDtypeStruct((4, 3, 8, LANES), F32),) * 2,
        scratch_shapes=[pltpu.VMEM((tiles, 4 * BLOCKS, LANES), F32)],
        cost_estimate=pl.CostEstimate(
            flops=5 * 10**8, bytes_accessed=2 * 10**6, transcendentals=0
        ),
        compiler_params=pltpu.CompilerParams(vmem_limit_bytes=VMEM_BYTES),
        name="bins_gram",
    )(where, coef.reshape(-1, LANES))


def norm_kernel(where_ref, r_ref, *refs):
    o_ref = refs[-1]
    total = r_ref[0]
    for z in range(1, 8):
        total = total + r_ref[z]
    for ref in refs[:-1]:
        total = total + ref[...]
    row = lax.broadcasted_iota(jnp.int32, (8, LANES), 0)
    lane = lax.broadcasted_iota(jnp.int32, (8, LANES), 1)
    for b in range(2):
        mine = (row == where_ref[3]) & (lane // BLOCKS == b)
        energy = jnp.sum(jnp.where(mine, total[2], 0.0), keepdims=True)
        out = total[b] * (BLOCKS / energy)
        o_ref[b, 0] = out[:, :BLOCKS]
        o_ref[b, 1] = out[:, BLOCKS:]


def normalized(where, parts, others):
    vmem = pl.BlockSpec(memory_space=pltpu.VMEM)
    return pl.pallas_call(
        norm_kernel,
        in_specs=[pl.BlockSpec(memory_space=pltpu.SMEM)] + [vmem] * (1 + len(others)),
        out_specs=vmem,
        out_shape=jax.ShapeDtypeStruct((2, 2, 8, BLOCKS), F32),
        compiler_params=pltpu.CompilerParams(vmem_limit_bytes=VMEM_BYTES),
        name="normalize",
    )(where, parts, *others)


def by_y(d):
    return [(2 * y + c, 2 * ((y + d) % 4) + c) for y in range(4) for c in range(2)]


def by_x(d):
    return [(8 * x + z, 8 * ((x + d) % 4) + z) for x in range(4) for z in range(8)]


def sent_on(near, axis, pairs):
    return [near(0)] + [lax.ppermute(near(d), axis, pairs(d)) for d in range(1, 4)]


def over_space(near, far):
    far = lax.ppermute(far, "space", [(s, s ^ 1) for s in range(8)])
    return sent_on(lambda d: near[d] + far[d], "space", by_y)


def odd_blocks(snapshots, closing, tm, tm_count, first):
    middle = (first + snapshots.shape[1]) // 2
    low, high = halves(snapshots, first, middle)
    down = lax.ppermute(low, "tm", [(t, t - 1) for t in range(1, tm_count)])
    up = lax.ppermute(high, "tm", [(t, (t + 1) % tm_count) for t in range(tm_count)])

    def finish(down, up):
        after = jnp.where(tm == tm_count - 1, closing[:, first:middle], down)
        ending = jnp.where(tm == 0, closing[:, middle:], snapshots[:HOP, middle:])
        return jnp.concatenate(
            [
                jnp.concatenate([snapshots[HOP:, first:middle], after], axis=0),
                jnp.concatenate([up, ending], axis=0),
            ],
            axis=1,
        )

    return down, up, finish


def body(snapshots, closing, weights, bin_index):
    tm_count = lax.axis_size("tm")
    tm, space = lax.axis_index("tm"), lax.axis_index("space")
    where = jnp.stack([space // 2, space % 2, tm // 8, tm % 8]).astype(jnp.int32)
    first = tm_count * PTS_TM
    roots = jnp.sqrt(weights)[None, :]
    down, up, finish = odd_blocks(snapshots, closing, tm, tm_count, first)
    sent = turned(snapshots, roots, first).reshape(tm_count, PTS_TM, NFFT)
    samples = lax.all_to_all(sent, "tm", 0, 0, tiled=True)
    down, up, bin_index, closing = lax.optimization_barrier((down, up, bin_index, closing))
    table = table_rows(bin_index, NFFT)
    own_roots = lax.dynamic_slice(roots, (0, tm * PTS_TM), (1, PTS_TM))
    own_closing = lax.dynamic_slice(closing, (0, tm * PTS_TM), (HOP, PTS_TM)) * own_roots
    coef = coefs(table, roots, snapshots, finish(down, up), first)
    samples, coef, own_closing = lax.optimization_barrier((samples, coef, own_closing.T))
    by_bin = lax.all_to_all(coef, "tm", 0, 0, tiled=True)
    held = sum(over_space(*points_gram(where, table, samples, own_closing)))
    held = sum(sent_on(lambda d: held[d], "tm", by_x))
    traces = jnp.broadcast_to(held[16:], (8, 1, 8, LANES))
    held = jnp.concatenate([held[:16].reshape(8, 2, 8, LANES), traces], axis=1)
    by_bin, held = lax.optimization_barrier((by_bin, held))
    columns = [[8 * x + z for z in range(8)] for x in range(4)]
    others = lax.all_to_all(held, "tm", 0, 0, tiled=True, axis_index_groups=columns)
    return normalized(where, others, over_space(*bins_gram(where, by_bin)))


def solution(mesh):
    return jax.shard_map(
        body,
        mesh=mesh,
        in_specs=(P("tm", "space"), P(None, "space"), P("space"), P()),
        out_specs=P("tm", None, "space", None),
        check_vma=False,
    )
```

```python
import functools
import math

import jax
import jax.numpy as jnp
from jax import lax
from jax.experimental import pallas as pl
from jax.experimental.pallas import tpu as pltpu
from jax.sharding import PartitionSpec as P

NFFT = 256
NBINS = 64
HOP = NFFT // 2
BLOCKS = 64
LANES = 128
PTS_TM = 168
F32, BF16 = jnp.float32, jnp.bfloat16
VMEM_BYTES = 50 * 2**20
LONG = 4 * 10**11


def split(a):
    hi = a.astype(BF16)
    return hi, (a - hi.astype(F32)).astype(BF16)


def dot3(a, b, dims):
    dg = lambda u, v: lax.dot_general(u, v, (dims, ((), ())), preferred_element_type=F32)
    return dg(a[0], b[0]) + dg(a[0], b[1]) + dg(a[1], b[0])


NN, NT = ((1,), (0,)), ((1,), (1,))


def gram3(a):
    dg = lambda u, v: lax.dot_general(u, v, (NT, ((), ())), preferred_element_type=F32)
    mixed = dg(a[0], a[1])
    return dg(a[0], a[0]) + mixed + mixed.T


def table_rows(bin_index, length):
    sample = jnp.arange(length, dtype=jnp.int32)
    window = 0.5 - 0.5 * jnp.cos(2.0 * jnp.pi * sample.astype(F32) / length)
    turns = sample[None, :] * bin_index[:, None] % length
    angle = 2.0 * jnp.pi * turns.astype(F32) / length
    paired = jnp.stack([window * jnp.cos(angle), -window * jnp.sin(angle)], axis=1)
    return paired.reshape(2 * bin_index.shape[0], length)


def widest(cols, most):
    return max(n * LANES for n in range(1, most + 1) if cols % (n * LANES) == 0)


def turn_kernel(x_ref, w_ref, o_ref, in_ref, out_ref, in_sems, out_sems):
    step = in_ref.shape[2]
    steps = in_ref.shape[0]
    ins = [
        pltpu.make_async_copy(x_ref.at[:, pl.ds(n * step, step)], in_ref.at[n], in_sems.at[n])
        for n in range(steps)
    ]
    outs = [
        pltpu.make_async_copy(out_ref.at[n], o_ref.at[pl.ds(n * step, step)], out_sems.at[n])
        for n in range(steps)
    ]
    for copy in ins:
        copy.start()
    for n in range(steps):
        ins[n].wait()
        out_ref[n] = (in_ref[n] * w_ref[:, n * step : (n + 1) * step]).T
        outs[n].start()
    for copy in outs:
        copy.wait()


def turned(x, roots, cols):
    rows, step = x.shape[0], widest(cols, 6)
    hbm = pl.BlockSpec(memory_space=pl.ANY)
    return pl.pallas_call(
        turn_kernel,
        in_specs=[hbm, pl.BlockSpec(memory_space=pltpu.VMEM)],
        out_specs=hbm,
        out_shape=jax.ShapeDtypeStruct((cols, rows), F32),
        scratch_shapes=[
            pltpu.VMEM((cols // step, rows, step), F32),
            pltpu.VMEM((cols // step, step, rows), F32),
            pltpu.SemaphoreType.DMA((cols // step,)),
            pltpu.SemaphoreType.DMA((cols // step,)),
        ],
        cost_estimate=pl.CostEstimate(flops=0, bytes_accessed=8 * rows * cols, transcendentals=0),
        compiler_params=pltpu.CompilerParams(vmem_limit_bytes=VMEM_BYTES),
        name="turn_samples",
    )(x, roots)


def halves_kernel(first, middle, x_ref, low_ref, high_ref, sems):
    low = pltpu.make_async_copy(
        x_ref.at[pl.ds(0, HOP), pl.ds(first, middle - first)], low_ref, sems.at[0]
    )
    high = pltpu.make_async_copy(
        x_ref.at[pl.ds(HOP, HOP), pl.ds(middle, x_ref.shape[1] - middle)], high_ref, sems.at[1]
    )
    low.start()
    high.start()
    low.wait()
    high.wait()


def halves(x, first, middle):
    return pl.pallas_call(
        functools.partial(halves_kernel, first, middle),
        in_specs=[pl.BlockSpec(memory_space=pl.ANY)],
        out_specs=(pl.BlockSpec(memory_space=pltpu.VMEM),) * 2,
        out_shape=(
            jax.ShapeDtypeStruct((HOP, middle - first), F32),
            jax.ShapeDtypeStruct((HOP, x.shape[1] - middle), F32),
        ),
        scratch_shapes=[pltpu.SemaphoreType.DMA((2,))],
        compiler_params=pltpu.CompilerParams(vmem_limit_bytes=VMEM_BYTES),
        name="halo_halves",
    )(x)


def lane_tile(a, n):
    return a[:, n * LANES : (n + 1) * LANES]


def coef_kernel(t_ref, w_ref, x_ref, odd_ref, o_ref, s_ref):
    table = split(t_ref[...])
    tiles = s_ref.shape[0]
    for e, part in enumerate((x_ref, odd_ref)):
        got = dot3(table, split(part[...] * w_ref[...]), NN)
        for n in range(tiles):
            s_ref.at[n][pl.ds(e, 2 * NBINS, stride=2), :] = lane_tile(got, n)
    for n in range(tiles):
        o_ref[:, n] = s_ref[n].reshape(-1, 8, LANES)


def coefs(table, roots, x, odd, first):
    rows, cols = x.shape[0], x.shape[1] - first
    step = widest(math.gcd(first, cols), 6)
    return pl.pallas_call(
        coef_kernel,
        grid=(cols // step,),
        in_specs=[
            pl.BlockSpec((2 * NBINS, rows), lambda i: (0, 0)),
            pl.BlockSpec((1, step), lambda i: (0, first // step + i)),
            pl.BlockSpec((rows, step), lambda i: (0, first // step + i)),
            pl.BlockSpec((rows, step), lambda i: (0, i)),
        ],
        out_specs=pl.BlockSpec((NBINS // 2, step // LANES, 8, LANES), lambda i: (0, i, 0, 0)),
        out_shape=jax.ShapeDtypeStruct((NBINS // 2, cols // LANES, 8, LANES), F32),
        scratch_shapes=[pltpu.VMEM((step // LANES, 4 * NBINS, LANES), F32)],
        cost_estimate=pl.CostEstimate(
            flops=LONG, bytes_accessed=10 * rows * cols, transcendentals=0
        ),
        compiler_params=pltpu.CompilerParams(vmem_limit_bytes=VMEM_BYTES),
        name="coefs_by_bin",
    )(table, roots, x, odd)


def re_im(gram):
    half = gram.shape[0] // 2
    other = pltpu.roll(gram[half:], half, 1)
    lane = lax.broadcasted_iota(jnp.int32, other.shape, 1)
    return gram[:half] + jnp.where(lane < half, other, -other)


def diagonal(out):
    row = lax.broadcasted_iota(jnp.int32, out.shape, 0)
    lane = lax.broadcasted_iota(jnp.int32, out.shape, 1)
    return jnp.sum(jnp.where(row == lane, out, 0.0), axis=0, keepdims=True)


def two_traces(first, second):
    return diagonal(first) + pltpu.roll(diagonal(second), BLOCKS, 1)


def by_core(rows, core):
    for y in range(4):
        even, odd = rows[16 * y : 16 * y + 8], rows[16 * y + 8 : 16 * y + 16]
        yield y, jnp.where(core == 0, even, odd), jnp.where(core == 0, odd, even)


def points_kernel(where_ref, t_ref, x_ref, c_ref, near_ref, far_ref, s_ref):
    tm_count, pts = x_ref.shape[0], x_ref.shape[1]
    tiles = s_ref.shape[0]
    table = split(t_ref[...])
    blank = jnp.zeros((tiles * LANES - pts, NFFT), F32)

    def transform(j, samples):
        got = dot3(table, split(jnp.concatenate([samples, blank], axis=0)), NT)
        for n in range(tiles):
            s_ref.at[n][pl.ds(j, 2 * NBINS, stride=BLOCKS), :] = lane_tile(got, n)

    def both(t, following):
        x = x_ref[t]
        transform(2 * t, x)
        transform(2 * t + 1, jnp.concatenate([x[:, HOP:], following], axis=1))

    def four(i, carry):
        for n in range(4):
            both(4 * i + n, x_ref[4 * i + n + 1][:, :HOP])
        return carry

    lax.fori_loop(0, tm_count // 4 - 1, four, 0)
    for t in range(tm_count - 4, tm_count - 1):
        both(t, x_ref[t + 1][:, :HOP])
    both(tm_count - 1, c_ref[...])

    y_at, core, x_at = (where_ref[n] for n in range(3))

    def owner(t):
        xr = lax.rem(t // 8 - x_at + 4, 4)
        z = lax.rem(t, 8)
        outs = []
        for b in range(2):
            mine = pl.ds(pl.multiple_of(2 * BLOCKS * (2 * t + b), 2 * BLOCKS), 2 * BLOCKS)
            rows = split(jnp.concatenate([s_ref[n, mine] for n in range(tiles)], axis=1))
            outs.append(re_im(dot3(rows, rows, NT)))
        for b in range(2):
            for y, near, far in by_core(outs[b], core):
                yr = lax.rem(y - y_at + 4, 4)
                near_ref[yr, xr, 2 * z + b] = near
                far_ref[yr, xr, 2 * z + b] = far
        traces = two_traces(*outs)
        for y in range(4):
            near_ref[y, xr, 16, pl.ds(z, 1), :] = traces
            far_ref[y, xr, 16, pl.ds(z, 1), :] = traces

    def four_owners(i, carry):
        for n in range(4):
            owner(4 * i + n)
        return carry

    lax.fori_loop(0, tm_count // 4, four_owners, 0)


def points_gram(where, table, samples, closing):
    wide = -(-samples.shape[1] // NFFT) * NFFT
    vmem = pl.BlockSpec(memory_space=pltpu.VMEM)
    return pl.pallas_call(
        points_kernel,
        in_specs=[pl.BlockSpec(memory_space=pltpu.SMEM), vmem, vmem, vmem],
        out_specs=(vmem, vmem),
        out_shape=(jax.ShapeDtypeStruct((4, 4, 17, 8, LANES), F32),) * 2,
        scratch_shapes=[pltpu.VMEM((wide // LANES, 2 * NBINS * BLOCKS, LANES), F32)],
        cost_estimate=pl.CostEstimate(
            flops=6 * 10**9, bytes_accessed=20 * 10**6, transcendentals=0
        ),
        compiler_params=pltpu.CompilerParams(vmem_limit_bytes=VMEM_BYTES),
        name="points_gram",
    )(where, table, samples, closing)


def bins_kernel(where_ref, a_ref, near_ref, far_ref, s_ref):
    tiles = s_ref.shape[0]
    tm_count = a_ref.shape[0] // (8 * tiles)
    for n in range(tiles):
        for c in range(4):
            for e in range(2):
                got = a_ref[pl.ds(8 * n + 2 * c + e, tm_count, stride=8 * tiles), :]
                if e == 1 and n >= tiles // 2:
                    got = pltpu.roll(got, tm_count - 1, 0)
                s_ref.at[n][pl.ds(c * BLOCKS + e, tm_count, stride=2), :] = got
    outs = []
    for b in range(2):
        mine = pl.ds(2 * BLOCKS * b, 2 * BLOCKS)
        rows = split(jnp.concatenate([s_ref[n, mine] for n in range(tiles)], axis=1))
        outs.append(re_im(gram3(rows)))
    y_at, core = where_ref[0], where_ref[1]
    for b in range(2):
        for y, near, far in by_core(outs[b], core):
            yr = lax.rem(y - y_at + 4, 4)
            near_ref[yr, b] = near
            far_ref[yr, b] = far
    traces = jnp.broadcast_to(two_traces(*outs), (8, LANES))
    for y in range(4):
        near_ref[y, 2] = traces
        far_ref[y, 2] = traces


def bins_gram(where, coef):
    vmem = pl.BlockSpec(memory_space=pltpu.VMEM)
    tiles = coef.shape[1]
    return pl.pallas_call(
        bins_kernel,
        in_specs=[pl.BlockSpec(memory_space=pltpu.SMEM), vmem],
        out_specs=(vmem, vmem),
        out_shape=(jax.ShapeDtypeStruct((4, 3, 8, LANES), F32),) * 2,
        scratch_shapes=[pltpu.VMEM((tiles, 4 * BLOCKS, LANES), F32)],
        cost_estimate=pl.CostEstimate(
            flops=5 * 10**8, bytes_accessed=2 * 10**6, transcendentals=0
        ),
        compiler_params=pltpu.CompilerParams(vmem_limit_bytes=VMEM_BYTES),
        name="bins_gram",
    )(where, coef.reshape(-1, LANES))


def norm_kernel(where_ref, r_ref, *refs):
    o_ref = refs[-1]
    total = r_ref[0]
    for z in range(1, 8):
        total = total + r_ref[z]
    for ref in refs[:-1]:
        total = total + ref[...]
    row = lax.broadcasted_iota(jnp.int32, (8, LANES), 0)
    lane = lax.broadcasted_iota(jnp.int32, (8, LANES), 1)
    for b in range(2):
        mine = (row == where_ref[3]) & (lane // BLOCKS == b)
        energy = jnp.sum(jnp.where(mine, total[2], 0.0), keepdims=True)
        out = total[b] * (BLOCKS / energy)
        o_ref[b, 0] = out[:, :BLOCKS]
        o_ref[b, 1] = out[:, BLOCKS:]


def normalized(where, parts, others):
    vmem = pl.BlockSpec(memory_space=pltpu.VMEM)
    return pl.pallas_call(
        norm_kernel,
        in_specs=[pl.BlockSpec(memory_space=pltpu.SMEM)] + [vmem] * (1 + len(others)),
        out_specs=vmem,
        out_shape=jax.ShapeDtypeStruct((2, 2, 8, BLOCKS), F32),
        compiler_params=pltpu.CompilerParams(vmem_limit_bytes=VMEM_BYTES),
        name="normalize",
    )(where, parts, *others)


def by_y(d):
    return [(2 * y + c, 2 * ((y + d) % 4) + c) for y in range(4) for c in range(2)]


def by_x(d):
    return [(8 * x + z, 8 * ((x + d) % 4) + z) for x in range(4) for z in range(8)]


def sent_on(near, axis, pairs):
    return [near(0)] + [lax.ppermute(near(d), axis, pairs(d)) for d in range(1, 4)]


def over_space(near, far):
    far = lax.ppermute(far, "space", [(s, s ^ 1) for s in range(8)])
    return sent_on(lambda d: near[d] + far[d], "space", by_y)


def odd_blocks(snapshots, closing, tm, tm_count, first):
    middle = (first + snapshots.shape[1]) // 2
    low, high = halves(snapshots, first, middle)
    down = lax.ppermute(low, "tm", [(t, t - 1) for t in range(1, tm_count)])
    up = lax.ppermute(high, "tm", [(t, (t + 1) % tm_count) for t in range(tm_count)])

    def finish(down, up):
        after = jnp.where(tm == tm_count - 1, closing[:, first:middle], down)
        ending = jnp.where(tm == 0, closing[:, middle:], snapshots[:HOP, middle:])
        return jnp.concatenate(
            [
                jnp.concatenate([snapshots[HOP:, first:middle], after], axis=0),
                jnp.concatenate([up, ending], axis=0),
            ],
            axis=1,
        )

    return down, up, finish


def body(snapshots, closing, weights, bin_index):
    tm_count = lax.axis_size("tm")
    tm, space = lax.axis_index("tm"), lax.axis_index("space")
    where = jnp.stack([space // 2, space % 2, tm // 8, tm % 8]).astype(jnp.int32)
    first = tm_count * PTS_TM
    roots = jnp.sqrt(weights)[None, :]
    down, up, finish = odd_blocks(snapshots, closing, tm, tm_count, first)
    sent = turned(snapshots, roots, first).reshape(tm_count, PTS_TM, NFFT)
    samples = lax.all_to_all(sent, "tm", 0, 0, tiled=True)
    down, up, bin_index, closing = lax.optimization_barrier((down, up, bin_index, closing))
    table = table_rows(bin_index, NFFT)
    own_roots = lax.dynamic_slice(roots, (0, tm * PTS_TM), (1, PTS_TM))
    own_closing = lax.dynamic_slice(closing, (0, tm * PTS_TM), (HOP, PTS_TM)) * own_roots
    coef = coefs(table, roots, snapshots, finish(down, up), first)
    samples, coef, own_closing = lax.optimization_barrier((samples, coef, own_closing.T))
    by_bin = lax.all_to_all(coef, "tm", 0, 0, tiled=True)
    held = sum(over_space(*points_gram(where, table, samples, own_closing)))
    held = sum(sent_on(lambda d: held[d], "tm", by_x))
    traces = jnp.broadcast_to(held[16:], (8, 1, 8, LANES))
    held = jnp.concatenate([held[:16].reshape(8, 2, 8, LANES), traces], axis=1)
    by_bin, held = lax.optimization_barrier((by_bin, held))
    columns = [[8 * x + z for z in range(8)] for x in range(4)]
    others = lax.all_to_all(held, "tm", 0, 0, tiled=True, axis_index_groups=columns)
    return normalized(where, others, over_space(*bins_gram(where, by_bin)))


def solution(mesh):
    return jax.shard_map(
        body,
        mesh=mesh,
        in_specs=(P("tm", "space"), P(None, "space"), P("space"), P()),
        out_specs=P("tm", None, "space", None),
        check_vma=False,
    )
```
